32 devices in a mesh: slab: 4 (over y, x), mode: 8 (over z, core).
Axes of the slice: x: 2, y: 2, z: 4, core: 2. Of those that a mesh axis runs over, the one named last changes fastest.
Arguments:
- tensor: bfloat16 [512, 16384], P('mode', 'slab'), may hold values from -24 to 24, as said below
- start_block: float32 [512, 128], replicated, may hold values from -6 to 6
Outputs:
- basis_rows: float32 [512, 128], P('mode')
- core_coeffs: float32 [16384, 128], P(('slab', 'mode'))
The draws below stay inside these ranges and needn't reach their ends.
Inputs may be any that keep to these rules, and one draw needn't show every extreme that they name: `tensor`: entries of the unfolding; each is a row factor times a column factor times a bounded random term.
All inputs are finite; a program needn't handle non-finite values.
Results may differ from the reference program's by a relative error of at most 0.0029.
Values may be sent and summed in bfloat16 or wider, within the bound.
No kernel may reach another device: no remote copies, remote signals or barrier semaphores. Data moves between devices by JAX's collectives and lax.ppermute only.
A program may use at most 64 MiB of HBM per device.

```python
import jax
import jax.numpy as jnp
from jax import lax

M = 512
R = 128
COLS = 16384


def draw_tensor(key, part):
    keys = jax.random.split(jax.random.fold_in(key, 7), 3)
    row_scale = jnp.exp(jax.random.uniform(keys[0], (M, 1), jnp.float32) * jnp.log(2.0))
    ramp = jnp.exp(jnp.log(3.0) * jnp.arange(COLS, dtype=jnp.float32) / COLS)
    col_scale = 0.3 * ramp * jnp.exp(jax.random.uniform(keys[1], (COLS,), jnp.float32) * jnp.log(10.0 / 3.0))
    noise = jax.random.truncated_normal(keys[2], -4.0, 4.0, (M, COLS), jnp.float32)
    return (row_scale * col_scale[None, :] * noise).astype(jnp.bfloat16)


def gaussian(own_key, shape, width, bound, kind=jnp.bfloat16):
    return jnp.clip(width * jax.random.normal(own_key, shape, jnp.float32), -bound, bound).astype(kind)


def setup_inputs(seed: int = 0) -> dict:
    key_list = jax.random.split(jax.random.key(seed), 3)
    tensor = draw_tensor(jax.random.fold_in(key_list[2], 71), 0)
    start_block = gaussian(key_list[1], (M, R), 1.0, 6.0, jnp.float32)
    return {"tensor": tensor, "start_block": start_block}


highest = lax.Precision.HIGHEST
contract_cols = (((1,), (1,)), ((), ()))
contract_rows = (((0,), (0,)), ((), ()))

def orthonormal(image_block):
    small_gram = jnp.dot(image_block.T, image_block, precision=highest)
    factor = jnp.linalg.cholesky(small_gram)
    return lax.linalg.triangular_solve(factor, image_block, left_side=False, lower=True, transpose_a=True)

def reference(tensor, start_block):
    gram_total = lax.dot_general(tensor.astype(jnp.float32), tensor.astype(jnp.float32), contract_cols, preferred_element_type=jnp.float32)
    image_block = jnp.dot(gram_total, start_block, precision=highest)
    basis_rows = orthonormal(image_block)
    basis_low = basis_rows.astype(jnp.bfloat16)
    core_coeffs = lax.dot_general(tensor.astype(jnp.float32), basis_low.astype(jnp.float32), contract_rows, preferred_element_type=jnp.float32)
    return (basis_rows, core_coeffs)
```

```python
import functools

import jax
import jax.numpy as jnp
from jax import lax
from jax.experimental import pallas as pl
from jax.experimental.pallas import tpu as pltpu
from jax.sharding import PartitionSpec as P

highest = lax.Precision.HIGHEST
f32 = jnp.float32
bf16 = jnp.bfloat16
contract_rows = (((0,), (0,)), ((), ()))
contract_last = (((1,), (1,)), ((), ()))


def two_parts(value):
    high = value.astype(bf16)
    return high, (value - high.astype(f32)).astype(bf16)


def dot(lhs, rhs, dims):
    return lax.dot_general(lhs, rhs, dims, preferred_element_type=f32)


def in_vmem(count):
    return [pl.BlockSpec(memory_space=pltpu.VMEM)] * count


def inner_kernel(chips, start_ref, *refs):
    blocks, (inner_ref, held_ref) = refs[:chips], refs[chips:]
    mode_index = lax.axis_index("mode")
    chip, core = mode_index // 2, mode_index % 2
    rows = blocks[0].shape[0]
    starts = []
    for step in range(chips):
        source = lax.rem(chip + chips - step, chips)
        held_ref[pl.ds(pl.multiple_of(source * rows, rows), rows), :] = blocks[step][...]
        first = pl.multiple_of((source * 2 + core) * rows, rows)
        starts.append(start_ref[pl.ds(first, rows), :])
    ordered = jnp.concatenate([block[...] for block in blocks], axis=0)
    high, low = two_parts(jnp.concatenate(starts, axis=0))
    inner_ref[...] = dot(high, ordered, contract_rows) + dot(low, ordered, contract_rows)


def image_kernel(held_ref, own_ref, other_ref, image_ref):
    high, low = two_parts(own_ref[...] + other_ref[...])
    held = held_ref[...]
    image_ref[...] = dot(held, high, contract_last) + dot(held, low, contract_last)


def swap(value, axis, mask):
    count = lax.axis_size(axis)
    return lax.ppermute(value, axis, [(i, i ^ mask) for i in range(count)])


def add_four(value, axis, first, second):
    near = swap(value, axis, first)
    side = swap(value, axis, second)
    far = swap(value, axis, first ^ second)
    return (value + near) + (side + far)


def add_over(value, axis, masks):
    masks = list(masks)
    while len(masks) >= 2:
        value = add_four(value, axis, masks.pop(0), masks.pop(0))
    if masks:
        value = value + swap(value, axis, masks.pop())
    return value


def orthonormal(image_block):
    small_gram = jnp.dot(image_block.T, image_block, precision=highest)
    factor = jnp.linalg.cholesky(small_gram)
    return lax.linalg.triangular_solve(
        factor, image_block, left_side=False, lower=True, transpose_a=True
    )


def shards(tensor, start_block):
    row_count, slab_columns = tensor.shape
    slabs, modes = lax.axis_size("slab"), lax.axis_size("mode")
    chips = modes // 2
    chip_columns = slab_columns // chips
    own_columns = chip_columns // 2
    rank = start_block.shape[1]
    mode_index = lax.axis_index("mode")
    chip, core = mode_index // 2, mode_index % 2

    def chip_block(step):
        target = lax.rem(chip + step, chips)
        return lax.dynamic_slice_in_dim(tensor, target * chip_columns, chip_columns, 1)

    blocks = [chip_block(0)] + [None] * (chips - 1)
    for step in sorted(range(1, chips), key=lambda step: -min(step, chips - step)):
        pairs = [(i, (i + 2 * step) % modes) for i in range(modes)]
        blocks[step] = lax.ppermute(chip_block(step), "mode", pairs)

    held_rows = chips * row_count
    inner, held = pl.pallas_call(
        functools.partial(inner_kernel, chips),
        out_shape=(
            jax.ShapeDtypeStruct((rank, chip_columns), f32),
            jax.ShapeDtypeStruct((held_rows, chip_columns), bf16),
        ),
        in_specs=in_vmem(1 + chips),
        out_specs=tuple(in_vmem(2)),
    )(start_block, *blocks)
    inner_other = swap(inner, "mode", 1)
    own_half = lax.dynamic_slice_in_dim(held, core * own_columns, own_columns, 1)
    away_half = lax.dynamic_slice_in_dim(held, (1 - core) * own_columns, own_columns, 1)
    other_half = swap(away_half, "mode", 1)

    image = pl.pallas_call(
        image_kernel,
        out_shape=jax.ShapeDtypeStruct((held_rows, rank), f32),
        in_specs=in_vmem(3),
        out_specs=in_vmem(1)[0],
    )(held, inner, inner_other)
    slab_masks = [1 << bit for bit in range(slabs.bit_length() - 1)]
    chip_masks = [2 * ((2 << bit) - 1) for bit in range(chips.bit_length() - 1)]
    image = add_over(image, "slab", slab_masks)
    image = add_over(image, "mode", chip_masks)

    image_other = swap(image, "mode", 1)
    even = core == 0
    image_block = jnp.concatenate(
        [jnp.where(even, image, image_other), jnp.where(even, image_other, image)], axis=0
    )
    basis_full = orthonormal(image_block)
    basis_low = basis_full.astype(bf16)
    basis_rows = lax.dynamic_slice_in_dim(
        basis_full, core * held_rows + chip * row_count, row_count, 0
    )
    regrouped = jnp.concatenate(
        [jnp.where(even, own_half, other_half), jnp.where(even, other_half, own_half)], axis=0
    )
    core_coeffs = dot(regrouped, basis_low, contract_rows)
    return (basis_rows, core_coeffs)


def solution(mesh):
    placed = (P("mode", "slab"), P())
    return jax.shard_map(
        shards,
        mesh=mesh,
        in_specs=placed,
        out_specs=(P("mode", None), P(("slab", "mode"), None)),
        check_vma=False,
    )
```

```python
import functools

import jax
import jax.numpy as jnp
from jax import lax
from jax.experimental import pallas as pl
from jax.experimental.pallas import tpu as pltpu
from jax.sharding import PartitionSpec as P

highest = lax.Precision.HIGHEST
f32 = jnp.float32
bf16 = jnp.bfloat16
contract_rows = (((0,), (0,)), ((), ()))
contract_last = (((1,), (1,)), ((), ()))


def two_parts(value):
    high = value.astype(bf16)
    return high, (value - high.astype(f32)).astype(bf16)


def dot(lhs, rhs, dims):
    return lax.dot_general(lhs, rhs, dims, preferred_element_type=f32)


def in_vmem(count):
    return [pl.BlockSpec(memory_space=pltpu.VMEM)] * count


def inner_kernel(chips, start_ref, *refs):
    blocks, (inner_ref, held_ref) = refs[:chips], refs[chips:]
    mode_index = lax.axis_index("mode")
    chip, core = mode_index // 2, mode_index % 2
    rows = blocks[0].shape[0]
    starts = []
    for step in range(chips):
        source = lax.rem(chip + chips - step, chips)
        held_ref[pl.ds(pl.multiple_of(source * rows, rows), rows), :] = blocks[step][...]
        first = pl.multiple_of((source * 2 + core) * rows, rows)
        starts.append(start_ref[pl.ds(first, rows), :])
    ordered = jnp.concatenate([block[...] for block in blocks], axis=0)
    high, low = two_parts(jnp.concatenate(starts, axis=0))
    inner_ref[...] = dot(high, ordered, contract_rows) + dot(low, ordered, contract_rows)


def image_kernel(held_ref, own_ref, other_ref, image_ref):
    high, low = two_parts(own_ref[...] + other_ref[...])
    held = held_ref[...]
    image_ref[...] = dot(held, high, contract_last) + dot(held, low, contract_last)


def swap(value, axis, mask):
    count = lax.axis_size(axis)
    return lax.ppermute(value, axis, [(i, i ^ mask) for i in range(count)])


def add_four(value, axis, first, second):
    near = swap(value, axis, first)
    side = swap(value, axis, second)
    far = swap(value, axis, first ^ second)
    return (value + near) + (side + far)


def add_over(value, axis, masks):
    masks = list(masks)
    while len(masks) >= 2:
        value = add_four(value, axis, masks.pop(0), masks.pop(0))
    if masks:
        value = value + swap(value, axis, masks.pop())
    return value


def inverse_factor(gram):
    size, tile = gram.shape[0], 8
    lane = lax.broadcasted_iota(jnp.int32, (tile, size), 1)
    level = lax.broadcasted_iota(jnp.int32, (tile, size), 0)
    def column(rows, index):
        return jnp.broadcast_to(rows[:, index : index + 1], (tile, size))
    def spread(rows, index):
        return jnp.broadcast_to(rows[index : index + 1, :], (tile, size))
    rows = [gram[first : first + tile, :] for first in range(0, size, tile)]
    result = []
    for block in range(size // tile):
        base = block * tile
        inside = (lane >= base) & (lane < base + tile)
        columns = [column(rows[block], base + c) for c in range(tile)]
        panel = jnp.where(inside, jnp.where(lane - base == level, 1.0, 0.0), rows[block])
        pivots = jnp.ones((tile, size), f32)
        inverses, known = [], {}
        for t in range(tile):
            pivot = spread(columns[t], t)
            pivots = jnp.where(level == t, pivot, pivots)
            inverses.append(1.0 / pivot)
            ratio = jnp.where(level > t, columns[t], 0.0) * inverses[t]
            panel = panel - ratio * spread(panel, t)
            for c in range(t + 1, tile):
                known[t, c] = spread(columns[c], t)
                columns[c] = columns[c] - ratio * known[t, c]
        result.append(jnp.where(lane <= base + level, panel, 0.0) * lax.rsqrt(pivots))
        spreads = [spread(panel, t) for t in range(tile)]
        for below in range(block + 1, size // tile):
            columns = [column(rows[below], base + c) for c in range(tile)]
            row = jnp.where(inside, 0.0, rows[below])
            for t in range(tile):
                ratio = columns[t] * inverses[t]
                row = row - ratio * spreads[t]
                for c in range(t + 1, tile):
                    columns[c] = columns[c] - ratio * known[t, c]
            rows[below] = row
    return jnp.concatenate(result, axis=0)


def outputs_kernel(rows, image_ref, image_other_ref, own_ref, other_ref, basis_ref, core_ref):
    mode_index = lax.axis_index("mode")
    chip, even = mode_index // 2, mode_index % 2 == 0
    image, image_other = image_ref[...], image_other_ref[...]
    image_block = jnp.concatenate(
        [jnp.where(even, image, image_other), jnp.where(even, image_other, image)], axis=0
    )
    small_gram = lax.dot_general(
        image_block, image_block, contract_rows, precision=highest, preferred_element_type=f32
    )
    inverse = inverse_factor(small_gram)
    basis_full = lax.dot_general(
        image_block, inverse, contract_last, precision=highest, preferred_element_type=f32
    )
    held = image.shape[0]
    basis_own = jnp.where(even, basis_full[:held], basis_full[held:])
    basis_other = jnp.where(even, basis_full[held:], basis_full[:held])
    for place in range(held // rows):
        @pl.when(chip == place)
        def _():
            basis_ref[...] = basis_own[place * rows : (place + 1) * rows]
    core_ref[...] = dot(own_ref[...], basis_own.astype(bf16), contract_rows) + dot(
        other_ref[...], basis_other.astype(bf16), contract_rows
    )


def shards(tensor, start_block):
    row_count, slab_columns = tensor.shape
    slabs, modes = lax.axis_size("slab"), lax.axis_size("mode")
    chips = modes // 2
    chip_columns = slab_columns // chips
    own_columns = chip_columns // 2
    rank = start_block.shape[1]
    mode_index = lax.axis_index("mode")
    chip, core = mode_index // 2, mode_index % 2

    def chip_block(step):
        target = lax.rem(chip + step, chips)
        return lax.dynamic_slice_in_dim(tensor, target * chip_columns, chip_columns, 1)

    blocks = [chip_block(0)] + [None] * (chips - 1)
    for step in sorted(range(1, chips), key=lambda step: -min(step, chips - step)):
        pairs = [(i, (i + 2 * step) % modes) for i in range(modes)]
        blocks[step] = lax.ppermute(chip_block(step), "mode", pairs)

    held_rows = chips * row_count
    inner, held = pl.pallas_call(
        functools.partial(inner_kernel, chips),
        out_shape=(
            jax.ShapeDtypeStruct((rank, chip_columns), f32),
            jax.ShapeDtypeStruct((held_rows, chip_columns), bf16),
        ),
        in_specs=in_vmem(1 + chips),
        out_specs=tuple(in_vmem(2)),
    )(start_block, *blocks)
    inner_other = swap(inner, "mode", 1)
    own_half = lax.dynamic_slice_in_dim(held, core * own_columns, own_columns, 1)
    away_half = lax.dynamic_slice_in_dim(held, (1 - core) * own_columns, own_columns, 1)
    other_half = swap(away_half, "mode", 1)

    image = pl.pallas_call(
        image_kernel,
        out_shape=jax.ShapeDtypeStruct((held_rows, rank), f32),
        in_specs=in_vmem(3),
        out_specs=in_vmem(1)[0],
    )(held, inner, inner_other)
    slab_masks = [1 << bit for bit in range(slabs.bit_length() - 1)]
    chip_masks = [2 * ((2 << bit) - 1) for bit in range(chips.bit_length() - 1)]
    image = add_over(image, "slab", slab_masks)
    image = add_over(image, "mode", chip_masks)

    image_other = swap(image, "mode", 1)
    return pl.pallas_call(
        functools.partial(outputs_kernel, row_count),
        out_shape=(
            jax.ShapeDtypeStruct((row_count, rank), f32),
            jax.ShapeDtypeStruct((own_columns, rank), f32),
        ),
        in_specs=in_vmem(4),
        out_specs=tuple(in_vmem(2)),
    )(image, image_other, own_half, other_half)


def solution(mesh):
    placed = (P("mode", "slab"), P())
    return jax.shard_map(
        shards,
        mesh=mesh,
        in_specs=placed,
        out_specs=(P("mode", None), P(("slab", "mode"), None)),
        check_vma=False,
    )
```

```python
import functools

import jax
import jax.numpy as jnp
from jax import lax
from jax.experimental import pallas as pl
from jax.experimental.pallas import tpu as pltpu
from jax.sharding import PartitionSpec as P

highest = lax.Precision.HIGHEST
f32 = jnp.float32
bf16 = jnp.bfloat16
contract_rows = (((0,), (0,)), ((), ()))
contract_last = (((1,), (1,)), ((), ()))


def two_parts(value):
    high = value.astype(bf16)
    return high, (value - high.astype(f32)).astype(bf16)


def dot(lhs, rhs, dims):
    return lax.dot_general(lhs, rhs, dims, preferred_element_type=f32)


def in_vmem(*arrays):
    return [pltpu.with_memory_space_constraint(array, pltpu.VMEM) for array in arrays]


def vmem_specs(count):
    return [pl.BlockSpec(memory_space=pltpu.VMEM)] * count


def split_kernel(tensor_ref, *refs):
    blocks, semaphores = refs[:-1], refs[-1]
    chips = len(blocks)
    width = blocks[0].shape[1]
    chip = lax.axis_index("mode") // 2
    copies = []
    for step, block in enumerate(blocks):
        target = lax.rem(chip + step, chips)
        columns = pl.ds(pl.multiple_of(target * width, width), width)
        copies.append(
            pltpu.make_async_copy(tensor_ref.at[:, columns], block, semaphores.at[step])
        )
    for copy in copies:
        copy.start()
    for copy in copies:
        copy.wait()


def inner_kernel(chips, start_ref, *refs):
    blocks, (inner_ref, held_ref, own_ref, away_ref) = refs[:chips], refs[chips:]
    mode_index = lax.axis_index("mode")
    chip, core = mode_index // 2, mode_index % 2
    rows, width = blocks[0].shape
    half = width // 2
    starts = []
    for step in range(chips):
        source = lax.rem(chip + chips - step, chips)
        place = pl.ds(pl.multiple_of(source * rows, rows), rows)
        held_ref[place, :] = blocks[step][...]
        own_ref[place, :] = blocks[step][:, pl.ds(pl.multiple_of(core * half, half), half)]
        away_ref[place, :] = blocks[step][:, pl.ds(pl.multiple_of((1 - core) * half, half), half)]
        first = pl.multiple_of((source * 2 + core) * rows, rows)
        starts.append(start_ref[pl.ds(first, rows), :])
    ordered = jnp.concatenate([block[...] for block in blocks], axis=0)
    high, low = two_parts(jnp.concatenate(starts, axis=0))
    inner_ref[...] = dot(high, ordered, contract_rows) + dot(low, ordered, contract_rows)


def image_kernel(held_ref, own_ref, other_ref, image_ref):
    high, low = two_parts(own_ref[...] + other_ref[...])
    held = held_ref[...]
    image_ref[...] = dot(held, high, contract_last) + dot(held, low, contract_last)


def swap_cores(value):
    return lax.ppermute(value, "mode", [(i, i ^ 1) for i in range(lax.axis_size("mode"))])


def exchange(value, even_masks, odd_masks):
    slabs, modes = lax.axis_size("slab"), lax.axis_size("mode")
    pairs = []
    for slab in range(slabs):
        for mode in range(modes):
            slab_mask, chip_mask = odd_masks if mode % 2 else even_masks
            pairs.append((slab * modes + mode, (slab ^ slab_mask) * modes + (mode ^ 2 * chip_mask)))
    return lax.ppermute(value, ("slab", "mode"), pairs)


def both(first, second):
    return (first[0] ^ second[0], first[1] ^ second[1])


def sum_over_chips(value):
    slab_bits = lax.axis_size("slab").bit_length() - 1
    chip_bits = (lax.axis_size("mode") // 2).bit_length() - 1
    along_slab = [(1 << bit, 0) for bit in range(slab_bits)]
    along_mode = [(0, (2 << bit) - 1) for bit in range(chip_bits)]
    even, odd = along_slab + along_mode, along_mode + along_slab
    while len(even) >= 2:
        (a, b), (c, d) = even[:2], odd[:2]
        even, odd = even[2:], odd[2:]
        far = exchange(value, both(a, b), both(c, d))
        near = exchange(value, a, c)
        side = exchange(value, b, d)
        value = (value + near) + (side + far)
    if even:
        value = value + exchange(value, even[0], odd[0])
    return value


def inverse_factor(gram):
    size, tile = gram.shape[0], 8
    lane = lax.broadcasted_iota(jnp.int32, (tile, size), 1)
    level = lax.broadcasted_iota(jnp.int32, (tile, size), 0)
    def column(rows, index):
        return jnp.broadcast_to(rows[:, index : index + 1], (tile, size))
    def spread(rows, index):
        return jnp.broadcast_to(rows[index : index + 1, :], (tile, size))
    rows = [gram[first : first + tile, :] for first in range(0, size, tile)]
    result = []
    for block in range(size // tile):
        base = block * tile
        inside = (lane >= base) & (lane < base + tile)
        columns = [column(rows[block], base + c) for c in range(tile)]
        panel = jnp.where(inside, jnp.where(lane - base == level, 1.0, 0.0), rows[block])
        pivots = jnp.ones((tile, size), f32)
        inverses, known = [], {}
        for t in range(tile):
            pivot = spread(columns[t], t)
            pivots = jnp.where(level == t, pivot, pivots)
            inverses.append(1.0 / pivot)
            ratio = jnp.where(level > t, columns[t], 0.0) * inverses[t]
            panel = panel - ratio * spread(panel, t)
            for c in range(t + 1, tile):
                known[t, c] = spread(columns[c], t)
                columns[c] = columns[c] - ratio * known[t, c]
        result.append(jnp.where(lane <= base + level, panel, 0.0) * lax.rsqrt(pivots))
        spreads = [spread(panel, t) for t in range(tile)]
        for below in range(block + 1, size // tile):
            columns = [column(rows[below], base + c) for c in range(tile)]
            row = jnp.where(inside, 0.0, rows[below])
            for t in range(tile):
                ratio = columns[t] * inverses[t]
                row = row - ratio * spreads[t]
                for c in range(t + 1, tile):
                    columns[c] = columns[c] - ratio * known[t, c]
            rows[below] = row
    return jnp.concatenate(result, axis=0)


def outputs_kernel(rows, image_ref, image_other_ref, own_ref, other_ref, basis_ref, core_ref):
    mode_index = lax.axis_index("mode")
    chip, even = mode_index // 2, mode_index % 2 == 0
    image, image_other = image_ref[...], image_other_ref[...]
    image_block = jnp.concatenate(
        [jnp.where(even, image, image_other), jnp.where(even, image_other, image)], axis=0
    )
    small_gram = lax.dot_general(
        image_block, image_block, contract_rows, precision=highest, preferred_element_type=f32
    )
    inverse = inverse_factor(small_gram)
    basis_full = lax.dot_general(
        image_block, inverse, contract_last, precision=highest, preferred_element_type=f32
    )
    held = image.shape[0]
    basis_own = jnp.where(even, basis_full[:held], basis_full[held:])
    basis_other = jnp.where(even, basis_full[held:], basis_full[:held])
    for place in range(held // rows):
        @pl.when(chip == place)
        def _():
            basis_ref[...] = basis_own[place * rows : (place + 1) * rows]
    core_ref[...] = dot(own_ref[...], basis_own.astype(bf16), contract_rows) + dot(
        other_ref[...], basis_other.astype(bf16), contract_rows
    )


def shards(tensor, start_block):
    row_count, slab_columns = tensor.shape
    modes = lax.axis_size("mode")
    chips = modes // 2
    chip_columns = slab_columns // chips
    own_columns = chip_columns // 2
    held_rows = chips * row_count
    rank = start_block.shape[1]

    blocks = list(pl.pallas_call(
        split_kernel,
        out_shape=[pltpu.VMEM((row_count, chip_columns), bf16)] * chips,
        in_specs=[pl.BlockSpec(memory_space=pl.ANY)],
        out_specs=vmem_specs(chips),
        scratch_shapes=[pltpu.SemaphoreType.DMA((chips,))],
    )(tensor))
    for step in sorted(range(1, chips), key=lambda step: -min(step, chips - step)):
        pairs = [(i, (i + 2 * step) % modes) for i in range(modes)]
        blocks[step] = lax.ppermute(blocks[step], "mode", pairs)

    inner, held, own_half, away_half = pl.pallas_call(
        functools.partial(inner_kernel, chips),
        out_shape=(
            pltpu.VMEM((rank, chip_columns), f32),
            pltpu.VMEM((held_rows, chip_columns), bf16),
            pltpu.VMEM((held_rows, own_columns), bf16),
            pltpu.VMEM((held_rows, own_columns), bf16),
        ),
        in_specs=vmem_specs(1 + chips),
        out_specs=tuple(vmem_specs(4)),
    )(*in_vmem(start_block, *blocks))
    inner_other = swap_cores(inner)
    other_half = swap_cores(away_half)

    image = pl.pallas_call(
        image_kernel,
        out_shape=pltpu.VMEM((held_rows, rank), f32),
        in_specs=vmem_specs(3),
        out_specs=vmem_specs(1)[0],
    )(*in_vmem(held, inner, inner_other))
    image = sum_over_chips(image)
    image_other = swap_cores(image)

    return pl.pallas_call(
        functools.partial(outputs_kernel, row_count),
        out_shape=(
            jax.ShapeDtypeStruct((row_count, rank), f32),
            jax.ShapeDtypeStruct((own_columns, rank), f32),
        ),
        in_specs=vmem_specs(4),
        out_specs=tuple(vmem_specs(2)),
    )(*in_vmem(image, image_other, own_half, other_half))


def solution(mesh):
    placed = (P("mode", "slab"), P())
    return jax.shard_map(
        shards,
        mesh=mesh,
        in_specs=placed,
        out_specs=(P("mode", None), P(("slab", "mode"), None)),
        check_vma=False,
    )
```

```python
import functools

import jax
import jax.numpy as jnp
from jax import lax
from jax.experimental import pallas as pl
from jax.experimental.pallas import tpu as pltpu
from jax.sharding import PartitionSpec as P

highest = lax.Precision.HIGHEST
f32 = jnp.float32
bf16 = jnp.bfloat16
contract_rows = (((0,), (0,)), ((), ()))
contract_last = (((1,), (1,)), ((), ()))


def two_parts(value):
    high = value.astype(bf16)
    return high, (value - high.astype(f32)).astype(bf16)


def dot(lhs, rhs, dims):
    return lax.dot_general(lhs, rhs, dims, preferred_element_type=f32)


def in_vmem(*arrays):
    return [pltpu.with_memory_space_constraint(array, pltpu.VMEM) for array in arrays]


def vmem_specs(count):
    return [pl.BlockSpec(memory_space=pltpu.VMEM)] * count


def split_kernel(tensor_ref, *refs):
    blocks, semaphores = refs[:-1], refs[-1]
    chips = len(blocks)
    width = blocks[0].shape[1]
    chip = lax.axis_index("mode") // 2
    copies = []
    for step, block in enumerate(blocks):
        target = lax.rem(chip + step, chips)
        columns = pl.ds(pl.multiple_of(target * width, width), width)
        copies.append(
            pltpu.make_async_copy(tensor_ref.at[:, columns], block, semaphores.at[step])
        )
    for copy in copies:
        copy.start()
    for copy in copies:
        copy.wait()


def inner_kernel(chips, start_ref, *refs):
    blocks, (inner_ref, held_ref, own_ref, away_ref) = refs[:chips], refs[chips:]
    mode_index = lax.axis_index("mode")
    chip, core = mode_index // 2, mode_index % 2
    rows, width = blocks[0].shape
    half = width // 2
    starts = []
    for step in range(chips):
        source = lax.rem(chip + chips - step, chips)
        place = pl.ds(pl.multiple_of(source * rows, rows), rows)
        held_ref[place, :] = blocks[step][...]
        own_ref[place, :] = blocks[step][:, pl.ds(pl.multiple_of(core * half, half), half)]
        away_ref[place, :] = blocks[step][:, pl.ds(pl.multiple_of((1 - core) * half, half), half)]
        first = pl.multiple_of((source * 2 + core) * rows, rows)
        starts.append(start_ref[pl.ds(first, rows), :])
    ordered = jnp.concatenate([block[...] for block in blocks], axis=0)
    high, low = two_parts(jnp.concatenate(starts, axis=0))
    inner_ref[...] = dot(high, ordered, contract_rows) + dot(low, ordered, contract_rows)


def image_kernel(held_ref, own_ref, other_ref, image_ref):
    high, low = two_parts(own_ref[...] + other_ref[...])
    held = held_ref[...]
    image_ref[...] = dot(held, high, contract_last) + dot(held, low, contract_last)


def swap_cores(value):
    return lax.ppermute(value, "mode", [(i, i ^ 1) for i in range(lax.axis_size("mode"))])


def exchange(value, even_masks, odd_masks):
    slabs, modes = lax.axis_size("slab"), lax.axis_size("mode")
    pairs = []
    for slab in range(slabs):
        for mode in range(modes):
            slab_mask, chip_mask = odd_masks if mode % 2 else even_masks
            pairs.append((slab * modes + mode, (slab ^ slab_mask) * modes + (mode ^ 2 * chip_mask)))
    return lax.ppermute(value, ("slab", "mode"), pairs)


def both(first, second):
    return (first[0] ^ second[0], first[1] ^ second[1])


def sum_over_chips(value):
    slab_bits = lax.axis_size("slab").bit_length() - 1
    chip_bits = (lax.axis_size("mode") // 2).bit_length() - 1
    along_slab = [(1 << bit, 0) for bit in range(slab_bits)]
    along_mode = [(0, (2 << bit) - 1) for bit in range(chip_bits)]
    even, odd = along_slab + along_mode, along_mode + along_slab
    while len(even) >= 2:
        (a, b), (c, d) = even[:2], odd[:2]
        even, odd = even[2:], odd[2:]
        far = exchange(value, both(a, b), both(c, d))
        near = exchange(value, a, c)
        side = exchange(value, b, d)
        value = (value + near) + (side + far)
    if even:
        value = value + exchange(value, even[0], odd[0])
    return value


def inverse_factor(gram):
    size, tile = gram.shape[0], 8
    count = size // tile
    span = max(count // 2, 1)
    lane = lax.broadcasted_iota(jnp.int32, (tile, size), 1)
    level = lax.broadcasted_iota(jnp.int32, (tile, size), 0)

    def columns(rows, base):
        return [jnp.broadcast_to(rows[:, c : c + 1], (tile, size)) for c in range(base, base + tile)]

    def spread(rows, index):
        return jnp.broadcast_to(rows[index : index + 1, :], (tile, size))

    rows = [gram[first : first + tile, :] for first in range(0, size, tile)]
    panels, scales = [None] * count, [None] * count
    ahead = None
    for start in range(0, count, span):
        stop = min(start + span, count)
        for block in range(start, stop):
            base = block * tile
            inside = (lane >= base) & (lane < base + tile)
            diagonal = ahead if block > start else columns(rows[block], base)
            follow = block + 1 < stop
            if follow:
                beside = columns(rows[block], base + tile)
                under = columns(rows[block + 1], base)
                ahead = columns(rows[block + 1], base + tile)
            pivots = jnp.ones((tile, size), f32)
            inverses, ratios, known = [], [], {}
            for t in range(tile):
                pivot = spread(diagonal[t], t)
                pivots = jnp.where(level == t, pivot, pivots)
                inverses.append(1.0 / pivot)
                ratios.append(jnp.where(level > t, diagonal[t], 0.0) * inverses[t])
                for c in range(t + 1, tile):
                    known[t, c] = spread(diagonal[c], t)
                    diagonal[c] = diagonal[c] - ratios[t] * known[t, c]
            if follow:
                for t in range(tile):
                    ratio = under[t] * inverses[t]
                    for c in range(t + 1, tile):
                        under[c] = under[c] - ratio * known[t, c]
                    for c in range(tile):
                        across = spread(beside[c], t)
                        ahead[c] = ahead[c] - ratio * across
                        beside[c] = beside[c] - ratios[t] * across
            panel = jnp.where(inside, jnp.where(lane - base == level, 1.0, 0.0), rows[block])
            spreads = []
            for t in range(tile):
                spreads.append(spread(panel, t))
                panel = panel - ratios[t] * spreads[t]
            panels[block], scales[block] = panel, pivots
            for below in range(block + 1, stop):
                multiples = columns(rows[below], base)
                row = jnp.where(inside, 0.0, rows[below])
                for t in range(tile):
                    ratio = multiples[t] * inverses[t]
                    row = row - ratio * spreads[t]
                    for c in range(t + 1, tile):
                        multiples[c] = multiples[c] - ratio * known[t, c]
                rows[below] = row
        if stop < count:
            first, last = start * tile, stop * tile
            done = range(start, stop)
            wide = [
                jnp.where((lane < last) & (lane > b * tile + level), 0.0, panels[b]) for b in done
            ]
            scaled = [panels[b] / scales[b] for b in done]
            change = lax.dot_general(
                jnp.concatenate(scaled, axis=0),
                jnp.concatenate(wide, axis=0),
                contract_rows,
                precision=highest,
                preferred_element_type=f32,
            )
            for below in range(stop, count):
                kept = jnp.where((lane >= first) & (lane < last), 0.0, rows[below])
                rows[below] = kept - change[below * tile : (below + 1) * tile]
    return jnp.concatenate(
        [
            jnp.where(lane <= b * tile + level, panels[b], 0.0) * lax.rsqrt(scales[b])
            for b in range(count)
        ],
        axis=0,
    )


def outputs_kernel(rows, image_ref, image_other_ref, own_ref, other_ref, basis_ref, core_ref):
    mode_index = lax.axis_index("mode")
    chip, even = mode_index // 2, mode_index % 2 == 0
    image, image_other = image_ref[...], image_other_ref[...]
    image_block = jnp.concatenate(
        [jnp.where(even, image, image_other), jnp.where(even, image_other, image)], axis=0
    )
    small_gram = lax.dot_general(
        image_block, image_block, contract_rows, precision=highest, preferred_element_type=f32
    )
    inverse = inverse_factor(small_gram)
    basis_full = lax.dot_general(
        image_block, inverse, contract_last, precision=highest, preferred_element_type=f32
    )
    held = image.shape[0]
    basis_own = jnp.where(even, basis_full[:held], basis_full[held:])
    basis_other = jnp.where(even, basis_full[held:], basis_full[:held])
    for place in range(held // rows):
        @pl.when(chip == place)
        def _():
            basis_ref[...] = basis_own[place * rows : (place + 1) * rows]
    core_ref[...] = dot(own_ref[...], basis_own.astype(bf16), contract_rows) + dot(
        other_ref[...], basis_other.astype(bf16), contract_rows
    )


def shards(tensor, start_block):
    row_count, slab_columns = tensor.shape
    modes = lax.axis_size("mode")
    chips = modes // 2
    chip_columns = slab_columns // chips
    own_columns = chip_columns // 2
    held_rows = chips * row_count
    rank = start_block.shape[1]

    blocks = list(pl.pallas_call(
        split_kernel,
        out_shape=[pltpu.VMEM((row_count, chip_columns), bf16)] * chips,
        in_specs=[pl.BlockSpec(memory_space=pl.ANY)],
        out_specs=vmem_specs(chips),
        scratch_shapes=[pltpu.SemaphoreType.DMA((chips,))],
    )(tensor))
    for step in sorted(range(1, chips), key=lambda step: -min(step, chips - step)):
        pairs = [(i, (i + 2 * step) % modes) for i in range(modes)]
        blocks[step] = lax.ppermute(blocks[step], "mode", pairs)

    inner, held, own_half, away_half = pl.pallas_call(
        functools.partial(inner_kernel, chips),
        out_shape=(
            pltpu.VMEM((rank, chip_columns), f32),
            pltpu.VMEM((held_rows, chip_columns), bf16),
            pltpu.VMEM((held_rows, own_columns), bf16),
            pltpu.VMEM((held_rows, own_columns), bf16),
        ),
        in_specs=vmem_specs(1 + chips),
        out_specs=tuple(vmem_specs(4)),
    )(*in_vmem(start_block, *blocks))
    inner_other = swap_cores(inner)
    other_half = swap_cores(away_half)

    image = pl.pallas_call(
        image_kernel,
        out_shape=pltpu.VMEM((held_rows, rank), f32),
        in_specs=vmem_specs(3),
        out_specs=vmem_specs(1)[0],
    )(*in_vmem(held, inner, inner_other))
    image = sum_over_chips(image)
    image_other = swap_cores(image)

    return pl.pallas_call(
        functools.partial(outputs_kernel, row_count),
        out_shape=(
            jax.ShapeDtypeStruct((row_count, rank), f32),
            jax.ShapeDtypeStruct((own_columns, rank), f32),
        ),
        in_specs=vmem_specs(4),
        out_specs=tuple(vmem_specs(2)),
    )(*in_vmem(image, image_other, own_half, other_half))


def solution(mesh):
    placed = (P("mode", "slab"), P())
    return jax.shard_map(
        shards,
        mesh=mesh,
        in_specs=placed,
        out_specs=(P("mode", None), P(("slab", "mode"), None)),
        check_vma=False,
    )
```

```python
import functools

import jax
import jax.numpy as jnp
from jax import lax
from jax.experimental import pallas as pl
from jax.experimental.pallas import tpu as pltpu
from jax.sharding import PartitionSpec as P

highest = lax.Precision.HIGHEST
f32 = jnp.float32
bf16 = jnp.bfloat16
contract_rows = (((0,), (0,)), ((), ()))
contract_last = (((1,), (1,)), ((), ()))


def two_parts(value):
    high = value.astype(bf16)
    return high, (value - high.astype(f32)).astype(bf16)


def dot(lhs, rhs, dims):
    return lax.dot_general(lhs, rhs, dims, preferred_element_type=f32)


def in_vmem(*arrays):
    return [pltpu.with_memory_space_constraint(array, pltpu.VMEM) for array in arrays]


def vmem_specs(count):
    return [pl.BlockSpec(memory_space=pltpu.VMEM)] * count


def split_kernel(masks, tensor_ref, *refs):
    blocks, semaphores = refs[:-1], refs[-1]
    width = blocks[0].shape[1]
    chip = lax.axis_index("mode") // 2
    copies = []
    for place, (mask, block) in enumerate(zip(masks, blocks)):
        columns = pl.ds(pl.multiple_of((chip ^ mask) * width, width), width)
        copies.append(
            pltpu.make_async_copy(tensor_ref.at[:, columns], block, semaphores.at[place])
        )
    for copy in copies:
        copy.start()
    for copy in copies:
        copy.wait()


def inner_kernel(masks, start_ref, *refs):
    blocks, (inner_ref, held_ref, own_ref, away_ref) = refs[: len(masks)], refs[len(masks) :]
    mode_index = lax.axis_index("mode")
    chip, core = mode_index // 2, mode_index % 2
    rows, width = blocks[0].shape
    half = width // 2
    starts = []
    for mask, block in zip(masks, blocks):
        source = chip ^ mask
        place = pl.ds(pl.multiple_of(source * rows, rows), rows)
        held_ref[place, :] = block[...]
        own_ref[place, :] = block[:, pl.ds(pl.multiple_of(core * half, half), half)]
        away_ref[place, :] = block[:, pl.ds(pl.multiple_of((1 - core) * half, half), half)]
        first = pl.multiple_of((source * 2 + (core ^ (mask & 1))) * rows, rows)
        starts.append(start_ref[pl.ds(first, rows), :])
    ordered = jnp.concatenate([block[...] for block in blocks], axis=0)
    high, low = two_parts(jnp.concatenate(starts, axis=0))
    inner_ref[...] = dot(high, ordered, contract_rows) + dot(low, ordered, contract_rows)


def image_kernel(held_ref, own_ref, other_ref, image_ref):
    high, low = two_parts(own_ref[...] + other_ref[...])
    held = held_ref[...]
    image_ref[...] = dot(held, high, contract_last) + dot(held, low, contract_last)


def swap_cores(value):
    return lax.ppermute(value, "mode", [(i, i ^ 1) for i in range(lax.axis_size("mode"))])


def exchange(value, even_masks, odd_masks):
    slabs, modes = lax.axis_size("slab"), lax.axis_size("mode")
    pairs = []
    for slab in range(slabs):
        for mode in range(modes):
            half = (mode % 2) ^ (mode // 2) % 2
            slab_mask, chip_mask = odd_masks if half else even_masks
            target = (slab ^ slab_mask) * modes + (mode ^ (2 * chip_mask + chip_mask % 2))
            pairs.append((slab * modes + mode, target))
    return lax.ppermute(value, ("slab", "mode"), pairs)


def both(first, second):
    return (first[0] ^ second[0], first[1] ^ second[1])


def sum_over_chips(value):
    slab_bits = lax.axis_size("slab").bit_length() - 1
    chip_bits = (lax.axis_size("mode") // 2).bit_length() - 1
    along_slab = [(1 << bit, 0) for bit in range(slab_bits)]
    along_mode = [(0, (2 << bit) - 1) for bit in range(chip_bits)]
    even, odd = along_slab + along_mode, along_mode + along_slab
    while len(even) >= 2:
        (a, b), (c, d) = even[:2], odd[:2]
        even, odd = even[2:], odd[2:]
        far = exchange(value, both(a, b), both(c, d))
        near = exchange(value, a, c)
        side = exchange(value, b, d)
        value = (value + near) + (side + far)
    if even:
        value = value + exchange(value, even[0], odd[0])
    return value


def inverse_factor(gram):
    size, tile = gram.shape[0], 8
    count = size // tile
    span = max(count // 2, 1)
    lane = lax.broadcasted_iota(jnp.int32, (tile, size), 1)
    level = lax.broadcasted_iota(jnp.int32, (tile, size), 0)

    def columns(rows, base):
        return [jnp.broadcast_to(rows[:, c : c + 1], (tile, size)) for c in range(base, base + tile)]

    def spread(rows, index):
        return jnp.broadcast_to(rows[index : index + 1, :], (tile, size))

    rows = [gram[first : first + tile, :] for first in range(0, size, tile)]
    panels, scales = [None] * count, [None] * count
    ahead = None
    for start in range(0, count, span):
        stop = min(start + span, count)
        for block in range(start, stop):
            base = block * tile
            inside = (lane >= base) & (lane < base + tile)
            diagonal = ahead if block > start else columns(rows[block], base)
            follow = block + 1 < stop
            if follow:
                beside = columns(rows[block], base + tile)
                under = columns(rows[block + 1], base)
                ahead = columns(rows[block + 1], base + tile)
            pivots = jnp.ones((tile, size), f32)
            inverses, ratios, known = [], [], {}
            for t in range(tile):
                pivot = spread(diagonal[t], t)
                pivots = jnp.where(level == t, pivot, pivots)
                inverses.append(1.0 / pivot)
                ratios.append(jnp.where(level > t, diagonal[t], 0.0) * inverses[t])
                for c in range(t + 1, tile):
                    known[t, c] = spread(diagonal[c], t)
                    diagonal[c] = diagonal[c] - ratios[t] * known[t, c]
            if follow:
                for t in range(tile):
                    ratio = under[t] * inverses[t]
                    for c in range(t + 1, tile):
                        under[c] = under[c] - ratio * known[t, c]
                    for c in range(tile):
                        across = spread(beside[c], t)
                        ahead[c] = ahead[c] - ratio * across
                        beside[c] = beside[c] - ratios[t] * across
            panel = jnp.where(inside, jnp.where(lane - base == level, 1.0, 0.0), rows[block])
            spreads = []
            for t in range(tile):
                spreads.append(spread(panel, t))
                panel = panel - ratios[t] * spreads[t]
            panels[block], scales[block] = panel, pivots
            for below in range(block + 1, stop):
                multiples = columns(rows[below], base)
                row = jnp.where(inside, 0.0, rows[below])
                for t in range(tile):
                    ratio = multiples[t] * inverses[t]
                    row = row - ratio * spreads[t]
                    for c in range(t + 1, tile):
                        multiples[c] = multiples[c] - ratio * known[t, c]
                rows[below] = row
        if stop < count:
            first, last = start * tile, stop * tile
            done = range(start, stop)
            wide = [
                jnp.where((lane < last) & (lane > b * tile + level), 0.0, panels[b]) for b in done
            ]
            scaled = [panels[b] / scales[b] for b in done]
            change = lax.dot_general(
                jnp.concatenate(scaled, axis=0),
                jnp.concatenate(wide, axis=0),
                contract_rows,
                precision=highest,
                preferred_element_type=f32,
            )
            for below in range(stop, count):
                kept = jnp.where((lane >= first) & (lane < last), 0.0, rows[below])
                rows[below] = kept - change[below * tile : (below + 1) * tile]
    return jnp.concatenate(
        [
            jnp.where(lane <= b * tile + level, panels[b], 0.0) * lax.rsqrt(scales[b])
            for b in range(count)
        ],
        axis=0,
    )


def outputs_kernel(image_ref, image_other_ref, own_ref, other_ref, basis_ref, core_ref, basis_own_ref):
    mode_index = lax.axis_index("mode")
    first = mode_index % 2 == mode_index // 2 % 2
    image, image_other = image_ref[...], image_other_ref[...]
    image_block = jnp.concatenate(
        [jnp.where(first, image, image_other), jnp.where(first, image_other, image)], axis=0
    )
    small_gram = lax.dot_general(
        image_block, image_block, contract_rows, precision=highest, preferred_element_type=f32
    )
    inverse = inverse_factor(small_gram)
    basis_own, basis_other = [
        lax.dot_general(part, inverse, contract_last, precision=highest, preferred_element_type=f32)
        for part in (image, image_other)
    ]
    basis_own_ref[...] = basis_own
    rows = basis_ref.shape[0]
    place = pl.multiple_of(mode_index // 2 * rows, rows)
    basis_ref[...] = basis_own_ref[pl.ds(place, rows), :]
    core_ref[...] = dot(own_ref[...], basis_own.astype(bf16), contract_rows) + dot(
        other_ref[...], basis_other.astype(bf16), contract_rows
    )


def in_chips(value, mask):
    flipped = 2 * mask + (mask & 1)
    return lax.ppermute(
        value, "mode", [(i, i ^ flipped) for i in range(lax.axis_size("mode"))]
    )


def shards(tensor, start_block):
    row_count, slab_columns = tensor.shape
    modes = lax.axis_size("mode")
    chips = modes // 2
    far_mask = chips // 2
    chip_columns = slab_columns // chips
    own_columns = chip_columns // 2
    held_rows = chips * row_count
    rank = start_block.shape[1]

    masks = [0, far_mask] + [mask for mask in reversed(range(1, chips)) if mask != far_mask]
    blocks = list(pl.pallas_call(
        functools.partial(split_kernel, masks),
        out_shape=[pltpu.VMEM((row_count, chip_columns), bf16)] * chips,
        in_specs=[pl.BlockSpec(memory_space=pl.ANY)],
        out_specs=vmem_specs(chips),
        scratch_shapes=[pltpu.SemaphoreType.DMA((chips,))],
    )(tensor))
    for place in range(1, chips):
        blocks[place] = in_chips(blocks[place], masks[place])

    inner, held, own_half, away_half = pl.pallas_call(
        functools.partial(inner_kernel, masks),
        out_shape=(
            pltpu.VMEM((rank, chip_columns), f32),
            pltpu.VMEM((held_rows, chip_columns), bf16),
            pltpu.VMEM((held_rows, own_columns), bf16),
            pltpu.VMEM((held_rows, own_columns), bf16),
        ),
        in_specs=vmem_specs(1 + chips),
        out_specs=tuple(vmem_specs(4)),
    )(*in_vmem(start_block, *blocks))
    inner_other = swap_cores(inner)
    other_half = swap_cores(away_half)

    image = pl.pallas_call(
        image_kernel,
        out_shape=pltpu.VMEM((held_rows, rank), f32),
        in_specs=vmem_specs(3),
        out_specs=vmem_specs(1)[0],
    )(*in_vmem(held, inner, inner_other))
    image = sum_over_chips(image)
    image_other = swap_cores(image)

    return pl.pallas_call(
        outputs_kernel,
        out_shape=(
            jax.ShapeDtypeStruct((row_count, rank), f32),
            jax.ShapeDtypeStruct((own_columns, rank), f32),
        ),
        in_specs=vmem_specs(4),
        out_specs=tuple(vmem_specs(2)),
        scratch_shapes=[pltpu.VMEM((held_rows, rank), f32)],
    )(*in_vmem(image, image_other, own_half, other_half))


def solution(mesh):
    placed = (P("mode", "slab"), P())
    return jax.shard_map(
        shards,
        mesh=mesh,
        in_specs=placed,
        out_specs=(P("mode", None), P(("slab", "mode"), None)),
        check_vma=False,
    )
```

```python
import functools

import jax
import jax.numpy as jnp
from jax import lax
from jax.experimental import pallas as pl
from jax.experimental.pallas import tpu as pltpu
from jax.sharding import PartitionSpec as P

highest = lax.Precision.HIGHEST
f32 = jnp.float32
bf16 = jnp.bfloat16
contract_rows = (((0,), (0,)), ((), ()))
contract_last = (((1,), (1,)), ((), ()))


def two_parts(value):
    high = value.astype(bf16)
    return high, (value - high.astype(f32)).astype(bf16)


def dot(lhs, rhs, dims):
    return lax.dot_general(lhs, rhs, dims, preferred_element_type=f32)


def in_vmem(*arrays):
    return [pltpu.with_memory_space_constraint(array, pltpu.VMEM) for array in arrays]


def vmem_specs(count):
    return [pl.BlockSpec(memory_space=pltpu.VMEM)] * count


def split_kernel(masks, tensor_ref, *refs):
    blocks, semaphores = refs[:-1], refs[-1]
    width = blocks[0].shape[1]
    chip = lax.axis_index("mode") // 2
    copies = []
    for place, (mask, block) in enumerate(zip(masks, blocks)):
        columns = pl.ds(pl.multiple_of((chip ^ mask) * width, width), width)
        copies.append(
            pltpu.make_async_copy(tensor_ref.at[:, columns], block, semaphores.at[place])
        )
    for copy in copies:
        copy.start()
    for copy in copies:
        copy.wait()


def inner_kernel(masks, start_ref, *refs):
    blocks, (inner_ref, held_ref, own_ref, away_ref) = refs[: len(masks)], refs[len(masks) :]
    mode_index = lax.axis_index("mode")
    chip, core = mode_index // 2, mode_index % 2
    rows, width = blocks[0].shape
    half = width // 2
    starts = []
    for mask, block in zip(masks, blocks):
        source = chip ^ mask
        place = pl.ds(pl.multiple_of(source * rows, rows), rows)
        held_ref[place, :] = block[...]
        own_ref[place, :] = block[:, pl.ds(pl.multiple_of(core * half, half), half)]
        away_ref[place, :] = block[:, pl.ds(pl.multiple_of((1 - core) * half, half), half)]
        first = pl.multiple_of((source * 2 + (core ^ (mask & 1))) * rows, rows)
        starts.append(start_ref[pl.ds(first, rows), :])
    ordered = jnp.concatenate([block[...] for block in blocks], axis=0)
    high, low = two_parts(jnp.concatenate(starts, axis=0))
    inner_ref[...] = dot(high, ordered, contract_rows) + dot(low, ordered, contract_rows)


def image_kernel(held_ref, own_ref, other_ref, image_ref):
    high, low = two_parts(own_ref[...] + other_ref[...])
    held = held_ref[...]
    image_ref[...] = dot(held, high, contract_last) + dot(held, low, contract_last)


def swap_cores(value):
    return lax.ppermute(value, "mode", [(i, i ^ 1) for i in range(lax.axis_size("mode"))])


def exchange(value, even_masks, odd_masks):
    slabs, modes = lax.axis_size("slab"), lax.axis_size("mode")
    pairs = []
    for slab in range(slabs):
        for mode in range(modes):
            half = (mode % 2) ^ (mode // 2) % 2
            slab_mask, chip_mask = odd_masks if half else even_masks
            target = (slab ^ slab_mask) * modes + (mode ^ (2 * chip_mask + chip_mask % 2))
            pairs.append((slab * modes + mode, target))
    return lax.ppermute(value, ("slab", "mode"), pairs)


def both(first, second):
    return (first[0] ^ second[0], first[1] ^ second[1])


def sum_over_chips(value):
    slab_bits = lax.axis_size("slab").bit_length() - 1
    chip_bits = (lax.axis_size("mode") // 2).bit_length() - 1
    along_slab = [(1 << bit, 0) for bit in range(slab_bits)]
    along_mode = [(0, (2 << bit) - 1) for bit in range(chip_bits)]
    even, odd = along_slab + along_mode, along_mode + along_slab
    while len(even) >= 2:
        (a, b), (c, d) = even[:2], odd[:2]
        even, odd = even[2:], odd[2:]
        far = exchange(value, both(a, b), both(c, d))
        near = exchange(value, a, c)
        side = exchange(value, b, d)
        value = (value + near) + (side + far)
    if even:
        value = value + exchange(value, even[0], odd[0])
    return value


def inverse_factor(gram):
    size, tile = gram.shape[0], 8
    count = size // tile
    span = max(count // 2, 1)
    lane = lax.broadcasted_iota(jnp.int32, (tile, size), 1)
    level = lax.broadcasted_iota(jnp.int32, (tile, size), 0)

    def columns(rows, base):
        return [jnp.broadcast_to(rows[:, c : c + 1], (tile, size)) for c in range(base, base + tile)]

    def spread(rows, index):
        return jnp.broadcast_to(rows[index : index + 1, :], (tile, size))

    rows = [gram[first : first + tile, :] for first in range(0, size, tile)]
    panels, scales = [None] * count, [None] * count
    ahead = None
    for start in range(0, count, span):
        stop = min(start + span, count)
        for block in range(start, stop):
            base = block * tile
            inside = (lane >= base) & (lane < base + tile)
            diagonal = ahead if block > start else columns(rows[block], base)
            follow = block + 1 < stop
            if follow:
                beside = columns(rows[block], base + tile)
                under = columns(rows[block + 1], base)
                ahead = columns(rows[block + 1], base + tile)
            pivots = jnp.ones((tile, size), f32)
            inverses, ratios, known = [], [], {}
            for t in range(tile):
                pivot = spread(diagonal[t], t)
                pivots = jnp.where(level == t, pivot, pivots)
                inverses.append(1.0 / pivot)
                ratios.append(jnp.where(level > t, diagonal[t], 0.0) * inverses[t])
                for c in range(t + 1, tile):
                    known[t, c] = spread(diagonal[c], t)
                    diagonal[c] = diagonal[c] - ratios[t] * known[t, c]
            if follow:
                for t in range(tile):
                    ratio = under[t] * inverses[t]
                    for c in range(t + 1, tile):
                        under[c] = under[c] - ratio * known[t, c]
                    for c in range(tile):
                        across = spread(beside[c], t)
                        ahead[c] = ahead[c] - ratio * across
                        beside[c] = beside[c] - ratios[t] * across
            panel = jnp.where(inside, jnp.where(lane - base == level, 1.0, 0.0), rows[block])
            spreads = []
            for t in range(tile):
                spreads.append(spread(panel, t))
                panel = panel - ratios[t] * spreads[t]
            panels[block], scales[block] = panel, pivots
            for below in range(block + 1, stop):
                multiples = columns(rows[below], base)
                row = jnp.where(inside, 0.0, rows[below])
                for t in range(tile):
                    ratio = multiples[t] * inverses[t]
                    row = row - ratio * spreads[t]
                    for c in range(t + 1, tile):
                        multiples[c] = multiples[c] - ratio * known[t, c]
                rows[below] = row
        if stop < count:
            first, last = start * tile, stop * tile
            done = range(start, stop)
            wide = [
                jnp.where((lane < last) & (lane > b * tile + level), 0.0, panels[b]) for b in done
            ]
            scaled = [panels[b] / scales[b] for b in done]
            change = lax.dot_general(
                jnp.concatenate(scaled, axis=0),
                jnp.concatenate(wide, axis=0),
                contract_rows,
                precision=highest,
                preferred_element_type=f32,
            )
            for below in range(stop, count):
                kept = jnp.where((lane >= first) & (lane < last), 0.0, rows[below])
                rows[below] = kept - change[below * tile : (below + 1) * tile]
    return jnp.concatenate(
        [
            jnp.where(lane <= b * tile + level, panels[b], 0.0) * lax.rsqrt(scales[b])
            for b in range(count)
        ],
        axis=0,
    )


def outputs_kernel(image_ref, image_other_ref, own_ref, other_ref, basis_ref, core_ref, basis_own_ref):
    mode_index = lax.axis_index("mode")
    first = mode_index % 2 == mode_index // 2 % 2
    image, image_other = image_ref[...], image_other_ref[...]
    image_block = jnp.concatenate(
        [jnp.where(first, image, image_other), jnp.where(first, image_other, image)], axis=0
    )
    small_gram = lax.dot_general(
        image_block, image_block, contract_rows, precision=highest, preferred_element_type=f32
    )
    inverse = inverse_factor(small_gram)
    basis_own, basis_other = [
        lax.dot_general(part, inverse, contract_last, precision=highest, preferred_element_type=f32)
        for part in (image, image_other)
    ]
    basis_own_ref[...] = basis_own
    rows = basis_ref.shape[0]
    place = pl.multiple_of(mode_index // 2 * rows, rows)
    basis_ref[...] = basis_own_ref[pl.ds(place, rows), :]
    core_ref[...] = dot(own_ref[...], basis_own.astype(bf16), contract_rows) + dot(
        other_ref[...], basis_other.astype(bf16), contract_rows
    )


def in_chips(value, mask):
    flipped = 2 * mask + (mask & 1)
    return lax.ppermute(
        value, "mode", [(i, i ^ flipped) for i in range(lax.axis_size("mode"))]
    )


def shards(tensor, start_block):
    row_count, slab_columns = tensor.shape
    modes = lax.axis_size("mode")
    chips = modes // 2
    far_mask = chips // 2
    chip_columns = slab_columns // chips
    own_columns = chip_columns // 2
    held_rows = chips * row_count
    rank = start_block.shape[1]

    masks = [0, far_mask] + [mask for mask in reversed(range(1, chips)) if mask != far_mask]
    def split(source, some):
        return pl.pallas_call(
            functools.partial(split_kernel, some),
            out_shape=[pltpu.VMEM((row_count, chip_columns), bf16)] * len(some),
            in_specs=[pl.BlockSpec(memory_space=pl.ANY)],
            out_specs=vmem_specs(len(some)),
            scratch_shapes=[pltpu.SemaphoreType.DMA((len(some),))],
        )(source)

    (far,) = split(tensor, [far_mask])
    far, tensor = lax.optimization_barrier((far, tensor))
    rest = split(tensor, [mask for mask in masks if mask != far_mask])
    blocks = [rest[0], far, *rest[1:]]
    for place in range(1, chips):
        blocks[place] = in_chips(blocks[place], masks[place])

    inner, held, own_half, away_half = pl.pallas_call(
        functools.partial(inner_kernel, masks),
        out_shape=(
            pltpu.VMEM((rank, chip_columns), f32),
            pltpu.VMEM((held_rows, chip_columns), bf16),
            pltpu.VMEM((held_rows, own_columns), bf16),
            pltpu.VMEM((held_rows, own_columns), bf16),
        ),
        in_specs=vmem_specs(1 + chips),
        out_specs=tuple(vmem_specs(4)),
    )(*in_vmem(start_block, *blocks))
    inner_other = swap_cores(inner)
    other_half = swap_cores(away_half)

    image = pl.pallas_call(
        image_kernel,
        out_shape=pltpu.VMEM((held_rows, rank), f32),
        in_specs=vmem_specs(3),
        out_specs=vmem_specs(1)[0],
    )(*in_vmem(held, inner, inner_other))
    image = sum_over_chips(image)
    image_other = swap_cores(image)

    return pl.pallas_call(
        outputs_kernel,
        out_shape=(
            jax.ShapeDtypeStruct((row_count, rank), f32),
            jax.ShapeDtypeStruct((own_columns, rank), f32),
        ),
        in_specs=vmem_specs(4),
        out_specs=tuple(vmem_specs(2)),
        scratch_shapes=[pltpu.VMEM((held_rows, rank), f32)],
    )(*in_vmem(image, image_other, own_half, other_half))


def solution(mesh):
    placed = (P("mode", "slab"), P())
    return jax.shard_map(
        shards,
        mesh=mesh,
        in_specs=placed,
        out_specs=(P("mode", None), P(("slab", "mode"), None)),
        check_vma=False,
    )
```

```python
import functools

import jax
import jax.numpy as jnp
from jax import lax
from jax.experimental import pallas as pl
from jax.experimental.pallas import tpu as pltpu
from jax.sharding import PartitionSpec as P

highest = lax.Precision.HIGHEST
f32 = jnp.float32
bf16 = jnp.bfloat16
contract_rows = (((0,), (0,)), ((), ()))
contract_last = (((1,), (1,)), ((), ()))


def two_parts(value):
    high = value.astype(bf16)
    return high, (value - high.astype(f32)).astype(bf16)


def dot(lhs, rhs, dims):
    return lax.dot_general(lhs, rhs, dims, preferred_element_type=f32)


def in_vmem(*arrays):
    return [pltpu.with_memory_space_constraint(array, pltpu.VMEM) for array in arrays]


def vmem_specs(count):
    return [pl.BlockSpec(memory_space=pltpu.VMEM)] * count


def split_kernel(masks, tensor_ref, *refs):
    blocks, semaphores = refs[:-1], refs[-1]
    width = blocks[0].shape[1]
    chip = lax.axis_index("mode") // 2
    copies = []
    for place, (mask, block) in enumerate(zip(masks, blocks)):
        columns = pl.ds(pl.multiple_of((chip ^ mask) * width, width), width)
        copies.append(
            pltpu.make_async_copy(tensor_ref.at[:, columns], block, semaphores.at[place])
        )
    for copy in copies:
        copy.start()
    for copy in copies:
        copy.wait()


def inner_kernel(masks, start_ref, *refs):
    blocks, (inner_ref, inner_low_ref, held_ref, own_ref, away_ref) = refs[: len(masks)], refs[len(masks) :]
    mode_index = lax.axis_index("mode")
    chip, core = mode_index // 2, mode_index % 2
    rows, width = blocks[0].shape
    half = width // 2
    starts = []
    for mask, block in zip(masks, blocks):
        source = chip ^ mask
        place = pl.ds(pl.multiple_of(source * rows, rows), rows)
        held_ref[place, :] = block[...]
        own_ref[place, :] = block[:, pl.ds(pl.multiple_of(core * half, half), half)]
        away_ref[place, :] = block[:, pl.ds(pl.multiple_of((1 - core) * half, half), half)]
        first = pl.multiple_of((source * 2 + (core ^ (mask & 1))) * rows, rows)
        starts.append(start_ref[pl.ds(first, rows), :])
    ordered = jnp.concatenate([block[...] for block in blocks], axis=0)
    high, low = two_parts(jnp.concatenate(starts, axis=0))
    inner = dot(high, ordered, contract_rows) + dot(low, ordered, contract_rows)
    inner_ref[...] = inner
    inner_low_ref[...] = inner.astype(bf16)


def image_kernel(held_ref, own_ref, other_ref, image_ref):
    high, low = two_parts(own_ref[...] + other_ref[...].astype(f32))
    held = held_ref[...]
    image = dot(held, high, contract_last) + dot(held, low, contract_last)
    image_ref[...] = image.astype(image_ref.dtype)


def swap_cores(value):
    return lax.ppermute(value, "mode", [(i, i ^ 1) for i in range(lax.axis_size("mode"))])


def exchange(value, even_masks, odd_masks):
    slabs, modes = lax.axis_size("slab"), lax.axis_size("mode")
    pairs = []
    for slab in range(slabs):
        for mode in range(modes):
            half = (mode % 2) ^ (mode // 2) % 2
            slab_mask, chip_mask = odd_masks if half else even_masks
            target = (slab ^ slab_mask) * modes + (mode ^ (2 * chip_mask + chip_mask % 2))
            pairs.append((slab * modes + mode, target))
    return lax.ppermute(value, ("slab", "mode"), pairs)


def both(first, second):
    return (first[0] ^ second[0], first[1] ^ second[1])


def sum_over_chips(value):
    slab_bits = lax.axis_size("slab").bit_length() - 1
    chip_bits = (lax.axis_size("mode") // 2).bit_length() - 1
    along_slab = [(1 << bit, 0) for bit in range(slab_bits)]
    along_mode = [(0, (2 << bit) - 1) for bit in range(chip_bits)]
    even, odd = along_slab + along_mode, along_mode + along_slab
    while len(even) >= 2:
        (a, b), (c, d) = even[:2], odd[:2]
        even, odd = even[2:], odd[2:]
        far = exchange(value, both(a, b), both(c, d)).astype(f32)
        near = exchange(value, a, c).astype(f32)
        side = exchange(value, b, d).astype(f32)
        value = (value.astype(f32) + near) + (side + far)
    if even:
        value = value.astype(f32) + exchange(value, even[0], odd[0]).astype(f32)
    return value


def inverse_factor(gram):
    size, tile = gram.shape[0], 8
    count = size // tile
    span = max(count // 2, 1)
    lane = lax.broadcasted_iota(jnp.int32, (tile, size), 1)
    level = lax.broadcasted_iota(jnp.int32, (tile, size), 0)

    def columns(rows, base):
        return [jnp.broadcast_to(rows[:, c : c + 1], (tile, size)) for c in range(base, base + tile)]

    def spread(rows, index):
        return jnp.broadcast_to(rows[index : index + 1, :], (tile, size))

    rows = [gram[first : first + tile, :] for first in range(0, size, tile)]
    panels, scales = [None] * count, [None] * count
    ahead = None
    for start in range(0, count, span):
        stop = min(start + span, count)
        for block in range(start, stop):
            base = block * tile
            inside = (lane >= base) & (lane < base + tile)
            diagonal = ahead if block > start else columns(rows[block], base)
            follow = block + 1 < stop
            if follow:
                beside = columns(rows[block], base + tile)
                under = columns(rows[block + 1], base)
                ahead = columns(rows[block + 1], base + tile)
            pivots = jnp.ones((tile, size), f32)
            inverses, ratios, known = [], [], {}
            for t in range(tile):
                pivot = spread(diagonal[t], t)
                pivots = jnp.where(level == t, pivot, pivots)
                inverses.append(1.0 / pivot)
                ratios.append(jnp.where(level > t, diagonal[t], 0.0) * inverses[t])
                for c in range(t + 1, tile):
                    known[t, c] = spread(diagonal[c], t)
                    diagonal[c] = diagonal[c] - ratios[t] * known[t, c]
            if follow:
                for t in range(tile):
                    ratio = under[t] * inverses[t]
                    for c in range(t + 1, tile):
                        under[c] = under[c] - ratio * known[t, c]
                    for c in range(tile):
                        across = spread(beside[c], t)
                        ahead[c] = ahead[c] - ratio * across
                        beside[c] = beside[c] - ratios[t] * across
            panel = jnp.where(inside, jnp.where(lane - base == level, 1.0, 0.0), rows[block])
            spreads = []
            for t in range(tile):
                spreads.append(spread(panel, t))
                panel = panel - ratios[t] * spreads[t]
            panels[block], scales[block] = panel, pivots
            for below in range(block + 1, stop):
                multiples = columns(rows[below], base)
                row = jnp.where(inside, 0.0, rows[below])
                for t in range(tile):
                    ratio = multiples[t] * inverses[t]
                    row = row - ratio * spreads[t]
                    for c in range(t + 1, tile):
                        multiples[c] = multiples[c] - ratio * known[t, c]
                rows[below] = row
        if stop < count:
            first, last = start * tile, stop * tile
            done = range(start, stop)
            wide = [
                jnp.where((lane < last) & (lane > b * tile + level), 0.0, panels[b]) for b in done
            ]
            scaled = [panels[b] / scales[b] for b in done]
            change = lax.dot_general(
                jnp.concatenate(scaled, axis=0),
                jnp.concatenate(wide, axis=0),
                contract_rows,
                precision=highest,
                preferred_element_type=f32,
            )
            for below in range(stop, count):
                kept = jnp.where((lane >= first) & (lane < last), 0.0, rows[below])
                rows[below] = kept - change[below * tile : (below + 1) * tile]
    return jnp.concatenate(
        [
            jnp.where(lane <= b * tile + level, panels[b], 0.0) * lax.rsqrt(scales[b])
            for b in range(count)
        ],
        axis=0,
    )


def gram_of(rows):
    return lax.dot_general(
        rows, rows, contract_rows, precision=highest, preferred_element_type=f32
    )


def gram_kernel(image_ref, gram_ref):
    gram_ref[...] = gram_of(image_ref[...])


def outputs_kernel(
    gram_ref, image_ref, image_other_ref, own_ref, other_ref, basis_ref, core_ref, basis_own_ref
):
    mode_index = lax.axis_index("mode")
    image_other = image_other_ref[...]
    inverse = inverse_factor(gram_ref[...] + gram_of(image_other))
    inverse_high, inverse_low = two_parts(inverse)

    def basis_of(image):
        high, low = two_parts(image)
        small = dot(high, inverse_low, contract_last) + dot(low, inverse_high, contract_last)
        return dot(high, inverse_high, contract_last) + small

    basis_own = basis_of(image_ref[...])
    basis_own_ref[...] = basis_own
    rows = basis_ref.shape[0]
    place = pl.multiple_of(mode_index // 2 * rows, rows)
    basis_ref[...] = basis_own_ref[pl.ds(place, rows), :]
    core_ref[...] = dot(own_ref[...], basis_own.astype(bf16), contract_rows) + dot(
        other_ref[...], basis_of(image_other).astype(bf16), contract_rows
    )


def in_chips(value, mask):
    flipped = 2 * mask + (mask & 1)
    return lax.ppermute(
        value, "mode", [(i, i ^ flipped) for i in range(lax.axis_size("mode"))]
    )


def shards(tensor, start_block):
    row_count, slab_columns = tensor.shape
    modes = lax.axis_size("mode")
    chips = modes // 2
    far_mask = chips // 2
    chip_columns = slab_columns // chips
    own_columns = chip_columns // 2
    held_rows = chips * row_count
    rank = start_block.shape[1]

    masks = [0, far_mask] + [mask for mask in reversed(range(1, chips)) if mask != far_mask]
    def split(source, some):
        return pl.pallas_call(
            functools.partial(split_kernel, some),
            out_shape=[pltpu.VMEM((row_count, chip_columns), bf16)] * len(some),
            in_specs=[pl.BlockSpec(memory_space=pl.ANY)],
            out_specs=vmem_specs(len(some)),
            scratch_shapes=[pltpu.SemaphoreType.DMA((len(some),))],
        )(source)

    (far,) = split(tensor, [far_mask])
    far, tensor = lax.optimization_barrier((far, tensor))
    rest = split(tensor, [mask for mask in masks if mask != far_mask])
    blocks = [rest[0], far, *rest[1:]]
    for place in range(1, chips):
        blocks[place] = in_chips(blocks[place], masks[place])

    inner, inner_low, held, own_half, away_half = pl.pallas_call(
        functools.partial(inner_kernel, masks),
        out_shape=(
            pltpu.VMEM((rank, chip_columns), f32),
            pltpu.VMEM((rank, chip_columns), bf16),
            pltpu.VMEM((held_rows, chip_columns), bf16),
            pltpu.VMEM((held_rows, own_columns), bf16),
            pltpu.VMEM((held_rows, own_columns), bf16),
        ),
        in_specs=vmem_specs(1 + chips),
        out_specs=tuple(vmem_specs(5)),
    )(*in_vmem(start_block, *blocks))
    inner_other = swap_cores(inner_low)
    other_half = swap_cores(away_half)

    image = pl.pallas_call(
        image_kernel,
        out_shape=pltpu.VMEM((held_rows, rank), bf16),
        in_specs=vmem_specs(3),
        out_specs=vmem_specs(1)[0],
    )(*in_vmem(held, inner, inner_other))
    image = sum_over_chips(image)
    image_other = swap_cores(image)
    gram = pl.pallas_call(
        gram_kernel,
        out_shape=pltpu.VMEM((rank, rank), f32),
        in_specs=vmem_specs(1),
        out_specs=vmem_specs(1)[0],
    )(*in_vmem(image))

    return pl.pallas_call(
        outputs_kernel,
        out_shape=(
            jax.ShapeDtypeStruct((row_count, rank), f32),
            jax.ShapeDtypeStruct((own_columns, rank), f32),
        ),
        in_specs=vmem_specs(5),
        out_specs=tuple(vmem_specs(2)),
        scratch_shapes=[pltpu.VMEM((held_rows, rank), f32)],
    )(*in_vmem(gram, image, image_other, own_half, other_half))


def solution(mesh):
    placed = (P("mode", "slab"), P())
    return jax.shard_map(
        shards,
        mesh=mesh,
        in_specs=placed,
        out_specs=(P("mode", None), P(("slab", "mode"), None)),
        check_vma=False,
    )
```

```python
import functools

import jax
import jax.numpy as jnp
from jax import lax
from jax.experimental import pallas as pl
from jax.experimental.pallas import tpu as pltpu
from jax.sharding import PartitionSpec as P

highest = lax.Precision.HIGHEST
f32 = jnp.float32
bf16 = jnp.bfloat16
contract_rows = (((0,), (0,)), ((), ()))
contract_last = (((1,), (1,)), ((), ()))


def two_parts(value):
    high = value.astype(bf16)
    return high, (value - high.astype(f32)).astype(bf16)


def dot(lhs, rhs, dims):
    return lax.dot_general(lhs, rhs, dims, preferred_element_type=f32)


def in_vmem(*arrays):
    return [pltpu.with_memory_space_constraint(array, pltpu.VMEM) for array in arrays]


def vmem_specs(count):
    return [pl.BlockSpec(memory_space=pltpu.VMEM)] * count


def chosen(masks):
    mode_index = lax.axis_index("mode")
    half = (mode_index // 2 + mode_index) % 2
    return masks[0] if masks[0] == masks[1] else jnp.where(half == 0, masks[0], masks[1])


def split_kernel(masks, tensor_ref, *refs):
    blocks, semaphores = refs[:-1], refs[-1]
    width = blocks[0].shape[1]
    chip = lax.axis_index("mode") // 2
    copies = []
    for place, (mask, block) in enumerate(zip(masks, blocks)):
        columns = pl.ds(pl.multiple_of((chip ^ chosen(mask)) * width, width), width)
        copies.append(
            pltpu.make_async_copy(tensor_ref.at[:, columns], block, semaphores.at[place])
        )
    for copy in copies:
        copy.start()
    for copy in copies:
        copy.wait()


def inner_kernel(masks, start_ref, *refs):
    blocks, (inner_ref, inner_low_ref, held_ref, own_ref, away_ref) = refs[: len(masks)], refs[len(masks) :]
    mode_index = lax.axis_index("mode")
    chip, core = mode_index // 2, mode_index % 2
    rows, width = blocks[0].shape
    half = width // 2
    starts = []
    for mask, block in zip(masks, blocks):
        mask = chosen(mask)
        source = chip ^ mask
        place = pl.ds(pl.multiple_of(source * rows, rows), rows)
        held_ref[place, :] = block[...]
        own_ref[place, :] = block[:, pl.ds(pl.multiple_of(core * half, half), half)]
        away_ref[place, :] = block[:, pl.ds(pl.multiple_of((1 - core) * half, half), half)]
        first = pl.multiple_of((source * 2 + (core ^ (mask & 1))) * rows, rows)
        starts.append(start_ref[pl.ds(first, rows), :])
    ordered = jnp.concatenate([block[...] for block in blocks], axis=0)
    high, low = two_parts(jnp.concatenate(starts, axis=0))
    inner = dot(high, ordered, contract_rows) + dot(low, ordered, contract_rows)
    inner_ref[...] = inner
    inner_low_ref[...] = inner.astype(bf16)


def image_kernel(held_ref, own_ref, other_ref, image_ref):
    high, low = two_parts(own_ref[...] + other_ref[...].astype(f32))
    held = held_ref[...]
    image = dot(held, high, contract_last) + dot(held, low, contract_last)
    image_ref[...] = image.astype(image_ref.dtype)


def swap_cores(value):
    return lax.ppermute(value, "mode", [(i, i ^ 1) for i in range(lax.axis_size("mode"))])


def exchange(value, even_masks, odd_masks):
    slabs, modes = lax.axis_size("slab"), lax.axis_size("mode")
    pairs = []
    for slab in range(slabs):
        for mode in range(modes):
            half = (mode % 2) ^ (mode // 2) % 2
            slab_mask, chip_mask = odd_masks if half else even_masks
            target = (slab ^ slab_mask) * modes + (mode ^ (2 * chip_mask + chip_mask % 2))
            pairs.append((slab * modes + mode, target))
    return lax.ppermute(value, ("slab", "mode"), pairs)


def both(first, second):
    return (first[0] ^ second[0], first[1] ^ second[1])


def sum_over_chips(value):
    slab_bits = lax.axis_size("slab").bit_length() - 1
    chip_bits = (lax.axis_size("mode") // 2).bit_length() - 1
    along_slab = [(1 << bit, 0) for bit in range(slab_bits)]
    along_mode = [(0, (2 << bit) - 1) for bit in range(chip_bits)]
    even, odd = along_slab + along_mode, along_mode + along_slab
    while len(even) >= 2:
        (a, b), (c, d) = even[:2], odd[:2]
        even, odd = even[2:], odd[2:]
        far = exchange(value, both(a, b), both(c, d)).astype(f32)
        near = exchange(value, a, c).astype(f32)
        side = exchange(value, b, d).astype(f32)
        value = ((value.astype(f32) + near) + (side + far)).astype(value.dtype if len(even) else f32)
    if even:
        value = value.astype(f32) + exchange(value, even[0], odd[0]).astype(f32)
    return value


def inverse_factor(gram):
    size, tile = gram.shape[0], 8
    count = size // tile
    span = max(count // 2, 1)
    lane = lax.broadcasted_iota(jnp.int32, (tile, size), 1)
    level = lax.broadcasted_iota(jnp.int32, (tile, size), 0)

    def columns(rows, base):
        return [jnp.broadcast_to(rows[:, c : c + 1], (tile, size)) for c in range(base, base + tile)]

    def spread(rows, index):
        return jnp.broadcast_to(rows[index : index + 1, :], (tile, size))

    rows = [gram[first : first + tile, :] for first in range(0, size, tile)]
    panels, scales = [None] * count, [None] * count
    ahead = None
    for start in range(0, count, span):
        stop = min(start + span, count)
        for block in range(start, stop):
            base = block * tile
            inside = (lane >= base) & (lane < base + tile)
            diagonal = ahead if block > start else columns(rows[block], base)
            follow = block + 1 < stop
            if follow:
                beside = columns(rows[block], base + tile)
                under = columns(rows[block + 1], base)
                ahead = columns(rows[block + 1], base + tile)
            pivots = jnp.ones((tile, size), f32)
            inverses, ratios, known = [], [], {}
            for t in range(tile):
                pivot = spread(diagonal[t], t)
                pivots = jnp.where(level == t, pivot, pivots)
                inverses.append(1.0 / pivot)
                ratios.append(jnp.where(level > t, diagonal[t], 0.0) * inverses[t])
                for c in range(t + 1, tile):
                    known[t, c] = spread(diagonal[c], t)
                    diagonal[c] = diagonal[c] - ratios[t] * known[t, c]
            if follow:
                for t in range(tile):
                    ratio = under[t] * inverses[t]
                    for c in range(t + 1, tile):
                        under[c] = under[c] - ratio * known[t, c]
                    for c in range(tile):
                        across = spread(beside[c], t)
                        ahead[c] = ahead[c] - ratio * across
                        beside[c] = beside[c] - ratios[t] * across
            panel = jnp.where(inside, jnp.where(lane - base == level, 1.0, 0.0), rows[block])
            spreads = []
            for t in range(tile):
                spreads.append(spread(panel, t))
                panel = panel - ratios[t] * spreads[t]
            panels[block], scales[block] = panel, pivots
            for below in range(block + 1, stop):
                multiples = columns(rows[below], base)
                row = jnp.where(inside, 0.0, rows[below])
                for t in range(tile):
                    ratio = multiples[t] * inverses[t]
                    row = row - ratio * spreads[t]
                    for c in range(t + 1, tile):
                        multiples[c] = multiples[c] - ratio * known[t, c]
                rows[below] = row
        if stop < count:
            first, last = start * tile, stop * tile
            done = range(start, stop)
            wide = [
                jnp.where((lane < last) & (lane > b * tile + level), 0.0, panels[b]) for b in done
            ]
            scaled = [panels[b] / scales[b] for b in done]
            change = lax.dot_general(
                jnp.concatenate(scaled, axis=0),
                jnp.concatenate(wide, axis=0),
                contract_rows,
                precision=highest,
                preferred_element_type=f32,
            )
            for below in range(stop, count):
                kept = jnp.where((lane >= first) & (lane < last), 0.0, rows[below])
                rows[below] = kept - change[below * tile : (below + 1) * tile]
    return jnp.concatenate(
        [
            jnp.where(lane <= b * tile + level, panels[b], 0.0) * lax.rsqrt(scales[b])
            for b in range(count)
        ],
        axis=0,
    )


def gram_of(rows):
    return lax.dot_general(
        rows, rows, contract_rows, precision=highest, preferred_element_type=f32
    )


def gram_kernel(image_ref, gram_ref):
    gram_ref[...] = gram_of(image_ref[...])


def outputs_kernel(
    gram_ref, image_ref, image_other_ref, own_ref, other_ref, basis_ref, core_ref, basis_own_ref
):
    mode_index = lax.axis_index("mode")
    image_other = image_other_ref[...]
    inverse = inverse_factor(gram_ref[...] + gram_of(image_other))
    inverse_high, inverse_low = two_parts(inverse)

    def basis_of(image):
        high, low = two_parts(image)
        small = dot(high, inverse_low, contract_last) + dot(low, inverse_high, contract_last)
        return dot(high, inverse_high, contract_last) + small

    basis_own = basis_of(image_ref[...])
    basis_own_ref[...] = basis_own
    rows = basis_ref.shape[0]
    place = pl.multiple_of(mode_index // 2 * rows, rows)
    basis_ref[...] = basis_own_ref[pl.ds(place, rows), :]
    core_ref[...] = dot(own_ref[...], basis_own.astype(bf16), contract_rows) + dot(
        other_ref[...], basis_of(image_other).astype(bf16), contract_rows
    )


def shards(tensor, start_block):
    row_count, slab_columns = tensor.shape
    modes = lax.axis_size("mode")
    chips = modes // 2
    far_mask = chips // 2
    chip_columns = slab_columns // chips
    own_columns = chip_columns // 2
    held_rows = chips * row_count
    rank = start_block.shape[1]

    last_mask = chips - 1
    masks = [(0, 0), (last_mask, far_mask), (far_mask, last_mask)]
    masks += [(mask, mask) for mask in range(1, chips) if mask not in (far_mask, last_mask)]

    def split(source, some):
        return pl.pallas_call(
            functools.partial(split_kernel, some),
            out_shape=[pltpu.VMEM((row_count, chip_columns), bf16)] * len(some),
            in_specs=[pl.BlockSpec(memory_space=pl.ANY)],
            out_specs=vmem_specs(len(some)),
            scratch_shapes=[pltpu.SemaphoreType.DMA((len(some),))],
        )(source)

    (first,) = split(tensor, masks[1:2])
    first, tensor = lax.optimization_barrier((first, tensor))
    rest = split(tensor, masks[:1] + masks[2:])
    blocks = [rest[0], first, *rest[1:]]
    for place in range(1, chips):
        even_mask, odd_mask = masks[place]
        blocks[place] = exchange(blocks[place], (0, even_mask), (0, odd_mask))

    inner, inner_low, held, own_half, away_half = pl.pallas_call(
        functools.partial(inner_kernel, masks),
        out_shape=(
            pltpu.VMEM((rank, chip_columns), f32),
            pltpu.VMEM((rank, chip_columns), bf16),
            pltpu.VMEM((held_rows, chip_columns), bf16),
            pltpu.VMEM((held_rows, own_columns), bf16),
            pltpu.VMEM((held_rows, own_columns), bf16),
        ),
        in_specs=vmem_specs(1 + chips),
        out_specs=tuple(vmem_specs(5)),
    )(*in_vmem(start_block, *blocks))
    inner_other = swap_cores(inner_low)
    other_half = swap_cores(away_half)

    image = pl.pallas_call(
        image_kernel,
        out_shape=pltpu.VMEM((held_rows, rank), bf16),
        in_specs=vmem_specs(3),
        out_specs=vmem_specs(1)[0],
    )(*in_vmem(held, inner, inner_other))
    image = sum_over_chips(image)
    image_other = swap_cores(image)
    gram = pl.pallas_call(
        gram_kernel,
        out_shape=pltpu.VMEM((rank, rank), f32),
        in_specs=vmem_specs(1),
        out_specs=vmem_specs(1)[0],
    )(*in_vmem(image))

    return pl.pallas_call(
        outputs_kernel,
        out_shape=(
            jax.ShapeDtypeStruct((row_count, rank), f32),
            jax.ShapeDtypeStruct((own_columns, rank), f32),
        ),
        in_specs=vmem_specs(5),
        out_specs=tuple(vmem_specs(2)),
        scratch_shapes=[pltpu.VMEM((held_rows, rank), f32)],
    )(*in_vmem(gram, image, image_other, own_half, other_half))


def solution(mesh):
    placed = (P("mode", "slab"), P())
    return jax.shard_map(
        shards,
        mesh=mesh,
        in_specs=placed,
        out_specs=(P("mode", None), P(("slab", "mode"), None)),
        check_vma=False,
    )
```

```python
import functools

import jax
import jax.numpy as jnp
from jax import lax
from jax.experimental import pallas as pl
from jax.experimental.pallas import tpu as pltpu
from jax.sharding import PartitionSpec as P

highest = lax.Precision.HIGHEST
f32 = jnp.float32
bf16 = jnp.bfloat16
contract_rows = (((0,), (0,)), ((), ()))
contract_last = (((1,), (1,)), ((), ()))


def two_parts(value):
    high = value.astype(bf16)
    return high, (value - high.astype(f32)).astype(bf16)


def dot(lhs, rhs, dims):
    return lax.dot_general(lhs, rhs, dims, preferred_element_type=f32)


def in_vmem(*arrays):
    return [pltpu.with_memory_space_constraint(array, pltpu.VMEM) for array in arrays]


def vmem_specs(count):
    return [pl.BlockSpec(memory_space=pltpu.VMEM)] * count


def chosen(masks):
    mode_index = lax.axis_index("mode")
    half = (mode_index // 2 + mode_index) % 2
    return masks[0] if masks[0] == masks[1] else jnp.where(half == 0, masks[0], masks[1])


def split_kernel(masks, tensor_ref, *refs):
    blocks, semaphores = refs[:-1], refs[-1]
    width = blocks[0].shape[1]
    chip = lax.axis_index("mode") // 2
    copies = []
    for place, (mask, block) in enumerate(zip(masks, blocks)):
        columns = pl.ds(pl.multiple_of((chip ^ chosen(mask)) * width, width), width)
        copies.append(
            pltpu.make_async_copy(tensor_ref.at[:, columns], block, semaphores.at[place])
        )
    for copy in copies:
        copy.start()
    for copy in copies:
        copy.wait()


def inner_kernel(masks, start_ref, *refs):
    blocks, (inner_ref, inner_low_ref, held_ref) = refs[: len(masks)], refs[len(masks) :]
    mode_index = lax.axis_index("mode")
    chip, core = mode_index // 2, mode_index % 2
    rows = blocks[0].shape[0]
    starts = []
    for mask, block in zip(masks, blocks):
        mask = chosen(mask)
        source = chip ^ mask
        place = pl.ds(pl.multiple_of(source * rows, rows), rows)
        held_ref[place, :] = block[...]
        first = pl.multiple_of((source * 2 + (core ^ (mask & 1))) * rows, rows)
        starts.append(start_ref[pl.ds(first, rows), :])
    ordered = jnp.concatenate([block[...] for block in blocks], axis=0)
    high, low = two_parts(jnp.concatenate(starts, axis=0))
    inner = dot(high, ordered, contract_rows) + dot(low, ordered, contract_rows)
    inner_ref[...] = inner
    inner_low_ref[...] = inner.astype(bf16)


def halves_kernel(held_ref, own_ref, away_ref):
    core, half = lax.axis_index("mode") % 2, own_ref.shape[1]
    own_ref[...] = held_ref[:, pl.ds(pl.multiple_of(core * half, half), half)]
    away_ref[...] = held_ref[:, pl.ds(pl.multiple_of((1 - core) * half, half), half)]


def image_kernel(held_ref, own_ref, other_ref, image_ref):
    high, low = two_parts(own_ref[...] + other_ref[...].astype(f32))
    held = held_ref[...]
    image = dot(held, high, contract_last) + dot(held, low, contract_last)
    image_ref[...] = image.astype(image_ref.dtype)


def swap_cores(value):
    return lax.ppermute(value, "mode", [(i, i ^ 1) for i in range(lax.axis_size("mode"))])


def exchange(value, even_masks, odd_masks):
    slabs, modes = lax.axis_size("slab"), lax.axis_size("mode")
    pairs = []
    for slab in range(slabs):
        for mode in range(modes):
            half = (mode % 2) ^ (mode // 2) % 2
            slab_mask, chip_mask = odd_masks if half else even_masks
            target = (slab ^ slab_mask) * modes + (mode ^ (2 * chip_mask + chip_mask % 2))
            pairs.append((slab * modes + mode, target))
    return lax.ppermute(value, ("slab", "mode"), pairs)


def add_kernel(value_ref, near_ref, side_ref, far_ref, total_ref):
    value, near, side, far = [
        ref[...].astype(f32) for ref in (value_ref, near_ref, side_ref, far_ref)
    ]
    total_ref[...] = ((value + near) + (side + far)).astype(total_ref.dtype)


def three_ways(first, second):
    sum_of_both = (first[0] ^ second[0], first[1] ^ second[1])
    along_slab = not (first[1] or second[1])
    return (second, first, sum_of_both) if along_slab else (first, sum_of_both, second)


def sum_over_chips(value):
    slab_bits = lax.axis_size("slab").bit_length() - 1
    chip_bits = (lax.axis_size("mode") // 2).bit_length() - 1
    along_slab = [(1 << bit, 0) for bit in range(slab_bits)]
    along_mode = [(0, (2 << bit) - 1) for bit in range(chip_bits)]
    even, odd = along_slab + along_mode, along_mode + along_slab
    while len(even) >= 2:
        ways = zip(three_ways(*even[:2]), three_ways(*odd[:2]))
        even, odd = even[2:], odd[2:]
        partners = [exchange(value, *masks) for masks in ways]
        value = pl.pallas_call(
            add_kernel,
            out_shape=pltpu.VMEM(value.shape, value.dtype if even else f32),
            in_specs=vmem_specs(4),
            out_specs=vmem_specs(1)[0],
        )(*in_vmem(value, *partners))
    if even:
        value = value.astype(f32) + exchange(value, even[0], odd[0]).astype(f32)
    return value


def inverse_factor(gram):
    size, tile = gram.shape[0], 8
    count = size // tile
    span = max(count // 2, 1)
    lane = lax.broadcasted_iota(jnp.int32, (tile, size), 1)
    level = lax.broadcasted_iota(jnp.int32, (tile, size), 0)

    def columns(rows, base):
        return [jnp.broadcast_to(rows[:, c : c + 1], (tile, size)) for c in range(base, base + tile)]

    def spread(rows, index):
        return jnp.broadcast_to(rows[index : index + 1, :], (tile, size))

    rows = [gram[first : first + tile, :] for first in range(0, size, tile)]
    panels, scales = [None] * count, [None] * count
    ahead = None
    for start in range(0, count, span):
        stop = min(start + span, count)
        for block in range(start, stop):
            base = block * tile
            inside = (lane >= base) & (lane < base + tile)
            diagonal = ahead if block > start else columns(rows[block], base)
            follow = block + 1 < stop
            if follow:
                beside = columns(rows[block], base + tile)
                under = columns(rows[block + 1], base)
                ahead = columns(rows[block + 1], base + tile)
            pivots = jnp.ones((tile, size), f32)
            inverses, ratios, known = [], [], {}
            for t in range(tile):
                pivot = spread(diagonal[t], t)
                pivots = jnp.where(level == t, pivot, pivots)
                inverses.append(1.0 / pivot)
                ratios.append(jnp.where(level > t, diagonal[t], 0.0) * inverses[t])
                for c in range(t + 1, tile):
                    known[t, c] = spread(diagonal[c], t)
                    diagonal[c] = diagonal[c] - ratios[t] * known[t, c]
            if follow:
                for t in range(tile):
                    ratio = under[t] * inverses[t]
                    for c in range(t + 1, tile):
                        under[c] = under[c] - ratio * known[t, c]
                    for c in range(tile):
                        across = spread(beside[c], t)
                        ahead[c] = ahead[c] - ratio * across
                        beside[c] = beside[c] - ratios[t] * across
            panel = jnp.where(inside, jnp.where(lane - base == level, 1.0, 0.0), rows[block])
            spreads = []
            for t in range(tile):
                spreads.append(spread(panel, t))
                panel = panel - ratios[t] * spreads[t]
            panels[block], scales[block] = panel, pivots
            for below in range(block + 1, stop):
                multiples = columns(rows[below], base)
                row = jnp.where(inside, 0.0, rows[below])
                for t in range(tile):
                    ratio = multiples[t] * inverses[t]
                    row = row - ratio * spreads[t]
                    for c in range(t + 1, tile):
                        multiples[c] = multiples[c] - ratio * known[t, c]
                rows[below] = row
        if stop < count:
            first, last = start * tile, stop * tile
            done = range(start, stop)
            wide = [
                jnp.where((lane < last) & (lane > b * tile + level), 0.0, panels[b]) for b in done
            ]
            scaled = [panels[b] / scales[b] for b in done]
            change = lax.dot_general(
                jnp.concatenate(scaled, axis=0),
                jnp.concatenate(wide, axis=0),
                contract_rows,
                precision=highest,
                preferred_element_type=f32,
            )
            for below in range(stop, count):
                kept = jnp.where((lane >= first) & (lane < last), 0.0, rows[below])
                rows[below] = kept - change[below * tile : (below + 1) * tile]
    return jnp.concatenate(
        [
            jnp.where(lane <= b * tile + level, panels[b], 0.0) * lax.rsqrt(scales[b])
            for b in range(count)
        ],
        axis=0,
    )


def gram_of(rows):
    return lax.dot_general(
        rows, rows, contract_rows, precision=highest, preferred_element_type=f32
    )


def gram_kernel(image_ref, gram_ref):
    gram_ref[...] = gram_of(image_ref[...])


def outputs_kernel(
    gram_ref, image_ref, image_other_ref, own_ref, other_ref, basis_ref, core_ref, basis_own_ref
):
    mode_index = lax.axis_index("mode")
    image_other = image_other_ref[...]
    inverse = inverse_factor(gram_ref[...] + gram_of(image_other))
    inverse_high, inverse_low = two_parts(inverse)

    def basis_of(image):
        high, low = two_parts(image)
        small = dot(high, inverse_low, contract_last) + dot(low, inverse_high, contract_last)
        return dot(high, inverse_high, contract_last) + small

    basis_own = basis_of(image_ref[...])
    basis_own_ref[...] = basis_own
    rows = basis_ref.shape[0]
    place = pl.multiple_of(mode_index // 2 * rows, rows)
    basis_ref[...] = basis_own_ref[pl.ds(place, rows), :]
    core_ref[...] = dot(own_ref[...], basis_own.astype(bf16), contract_rows) + dot(
        other_ref[...], basis_of(image_other).astype(bf16), contract_rows
    )


def shards(tensor, start_block):
    row_count, slab_columns = tensor.shape
    modes = lax.axis_size("mode")
    chips = modes // 2
    far_mask = chips // 2
    chip_columns = slab_columns // chips
    own_columns = chip_columns // 2
    held_rows = chips * row_count
    rank = start_block.shape[1]

    masks = [(0, 0), (far_mask, 1), (1, far_mask)] if far_mask > 1 else [(0, 0), (1, 1)]
    masks += [(mask, mask) for mask in reversed(range(2, chips)) if mask != far_mask]

    def split(source, some):
        return pl.pallas_call(
            functools.partial(split_kernel, some),
            out_shape=[pltpu.VMEM((row_count, chip_columns), bf16)] * len(some),
            in_specs=[pl.BlockSpec(memory_space=pl.ANY)],
            out_specs=vmem_specs(len(some)),
            scratch_shapes=[pltpu.SemaphoreType.DMA((len(some),))],
        )(source)

    (first,) = split(tensor, masks[1:2])
    first, tensor = lax.optimization_barrier((first, tensor))
    rest = split(tensor, masks[:1] + masks[2:])
    blocks = [rest[0], first, *rest[1:]]
    for place in range(1, chips):
        even_mask, odd_mask = masks[place]
        blocks[place] = exchange(blocks[place], (0, even_mask), (0, odd_mask))

    inner, inner_low, held = pl.pallas_call(
        functools.partial(inner_kernel, masks),
        out_shape=(
            pltpu.VMEM((rank, chip_columns), f32),
            pltpu.VMEM((rank, chip_columns), bf16),
            pltpu.VMEM((held_rows, chip_columns), bf16),
        ),
        in_specs=vmem_specs(1 + chips),
        out_specs=tuple(vmem_specs(3)),
    )(*in_vmem(start_block, *blocks))
    inner_other = swap_cores(inner_low)
    own_half, away_half = pl.pallas_call(
        halves_kernel,
        out_shape=(pltpu.VMEM((held_rows, own_columns), bf16),) * 2,
        in_specs=vmem_specs(1),
        out_specs=tuple(vmem_specs(2)),
    )(*in_vmem(held))
    other_half = swap_cores(away_half)

    image = pl.pallas_call(
        image_kernel,
        out_shape=pltpu.VMEM((held_rows, rank), bf16),
        in_specs=vmem_specs(3),
        out_specs=vmem_specs(1)[0],
    )(*in_vmem(held, inner, inner_other))
    image = sum_over_chips(image)
    image_other = swap_cores(image)
    gram = pl.pallas_call(
        gram_kernel,
        out_shape=pltpu.VMEM((rank, rank), f32),
        in_specs=vmem_specs(1),
        out_specs=vmem_specs(1)[0],
    )(*in_vmem(image))

    return pl.pallas_call(
        outputs_kernel,
        out_shape=(
            jax.ShapeDtypeStruct((row_count, rank), f32),
            jax.ShapeDtypeStruct((own_columns, rank), f32),
        ),
        in_specs=vmem_specs(5),
        out_specs=tuple(vmem_specs(2)),
        scratch_shapes=[pltpu.VMEM((held_rows, rank), f32)],
    )(*in_vmem(gram, image, image_other, own_half, other_half))


def solution(mesh):
    placed = (P("mode", "slab"), P())
    return jax.shard_map(
        shards,
        mesh=mesh,
        in_specs=placed,
        out_specs=(P("mode", None), P(("slab", "mode"), None)),
        check_vma=False,
    )
```

```python
import functools

import jax
import jax.numpy as jnp
from jax import lax
from jax.experimental import pallas as pl
from jax.experimental.pallas import tpu as pltpu
from jax.sharding import PartitionSpec as P

highest = lax.Precision.HIGHEST
f32 = jnp.float32
bf16 = jnp.bfloat16
contract_rows = (((0,), (0,)), ((), ()))
contract_last = (((1,), (1,)), ((), ()))


def two_parts(value):
    high = value.astype(bf16)
    return high, (value - high.astype(f32)).astype(bf16)


def dot(lhs, rhs, dims):
    return lax.dot_general(lhs, rhs, dims, preferred_element_type=f32)


def in_vmem(*arrays):
    return [pltpu.with_memory_space_constraint(array, pltpu.VMEM) for array in arrays]


def vmem_specs(count):
    return [pl.BlockSpec(memory_space=pltpu.VMEM)] * count


def chosen(masks):
    mode_index = lax.axis_index("mode")
    half = (mode_index // 2 + mode_index) % 2
    return masks[0] if masks[0] == masks[1] else jnp.where(half == 0, masks[0], masks[1])


def split_kernel(masks, tensor_ref, *refs):
    blocks, semaphores = refs[:-1], refs[-1]
    width = blocks[0].shape[1]
    chip = lax.axis_index("mode") // 2
    copies = []
    for mask, block in zip(masks, blocks):
        columns = pl.ds(pl.multiple_of((chip ^ chosen(mask)) * width, width), width)
        for first in range(0, block.shape[0], 16):
            rows = pl.ds(first, 16)
            copies.append(
                pltpu.make_async_copy(
                    tensor_ref.at[rows, columns], block.at[rows], semaphores.at[len(copies)]
                )
            )
    for copy in copies:
        copy.start()
    for copy in copies:
        copy.wait()


def inner_kernel(masks, start_ref, *refs):
    blocks, (inner_ref, inner_low_ref, held_ref, own_ref, away_ref) = refs[: len(masks)], refs[len(masks) :]
    mode_index = lax.axis_index("mode")
    chip, core = mode_index // 2, mode_index % 2
    rows, width = blocks[0].shape
    half = width // 2
    starts = []
    for mask, block in zip(masks, blocks):
        mask = chosen(mask)
        source = chip ^ mask
        place = pl.ds(pl.multiple_of(source * rows, rows), rows)
        held_ref[place, :] = block[...]
        own_ref[place, :] = block[:, pl.ds(pl.multiple_of(core * half, half), half)]
        away_ref[place, :] = block[:, pl.ds(pl.multiple_of((1 - core) * half, half), half)]
        first = pl.multiple_of((source * 2 + (core ^ (mask & 1))) * rows, rows)
        starts.append(start_ref[pl.ds(first, rows), :])
    ordered = jnp.concatenate([block[...] for block in blocks], axis=0)
    high, low = two_parts(jnp.concatenate(starts, axis=0))
    inner = dot(high, ordered, contract_rows) + dot(low, ordered, contract_rows)
    inner_ref[...] = inner
    inner_low_ref[...] = inner.astype(bf16)


def image_kernel(held_ref, own_ref, other_ref, image_ref):
    high, low = two_parts(own_ref[...] + other_ref[...].astype(f32))
    held = held_ref[...]
    image = dot(held, high, contract_last) + dot(held, low, contract_last)
    image_ref[...] = image.astype(image_ref.dtype)


def swap_cores(value):
    return lax.ppermute(value, "mode", [(i, i ^ 1) for i in range(lax.axis_size("mode"))])


def exchange(value, even_masks, odd_masks):
    slabs, modes = lax.axis_size("slab"), lax.axis_size("mode")
    pairs = []
    for slab in range(slabs):
        for mode in range(modes):
            half = (mode % 2) ^ (mode // 2) % 2
            slab_mask, chip_mask = odd_masks if half else even_masks
            target = (slab ^ slab_mask) * modes + (mode ^ (2 * chip_mask + chip_mask % 2))
            pairs.append((slab * modes + mode, target))
    return lax.ppermute(value, ("slab", "mode"), pairs)


def add_kernel(value_ref, near_ref, side_ref, far_ref, total_ref):
    value, near, side, far = [
        ref[...].astype(f32) for ref in (value_ref, near_ref, side_ref, far_ref)
    ]
    total_ref[...] = ((value + near) + (side + far)).astype(total_ref.dtype)


def three_ways(first, second):
    sum_of_both = (first[0] ^ second[0], first[1] ^ second[1])
    along_slab = not (first[1] or second[1])
    return (second, first, sum_of_both) if along_slab else (first, sum_of_both, second)


def sum_over_chips(value):
    slab_bits = lax.axis_size("slab").bit_length() - 1
    chip_bits = (lax.axis_size("mode") // 2).bit_length() - 1
    along_slab = [(1 << bit, 0) for bit in range(slab_bits)]
    along_mode = [(0, (2 << bit) - 1) for bit in range(chip_bits)]
    even, odd = along_slab + along_mode, along_mode + along_slab
    while len(even) >= 2:
        ways = zip(three_ways(*even[:2]), three_ways(*odd[:2]))
        even, odd = even[2:], odd[2:]
        partners = [exchange(value, *masks) for masks in ways]
        value = pl.pallas_call(
            add_kernel,
            out_shape=pltpu.VMEM(value.shape, value.dtype if even else f32),
            in_specs=vmem_specs(4),
            out_specs=vmem_specs(1)[0],
        )(*in_vmem(value, *partners))
    if even:
        value = value.astype(f32) + exchange(value, even[0], odd[0]).astype(f32)
    return value


def inverse_factor(gram):
    size, tile = gram.shape[0], 8
    count = size // tile
    span = max(count // 2, 1)
    lane = lax.broadcasted_iota(jnp.int32, (tile, size), 1)
    level = lax.broadcasted_iota(jnp.int32, (tile, size), 0)

    def columns(rows, base):
        return [jnp.broadcast_to(rows[:, c : c + 1], (tile, size)) for c in range(base, base + tile)]

    def spread(rows, index):
        return jnp.broadcast_to(rows[index : index + 1, :], (tile, size))

    rows = [gram[first : first + tile, :] for first in range(0, size, tile)]
    panels, scales = [None] * count, [None] * count
    ahead = None
    for start in range(0, count, span):
        stop = min(start + span, count)
        for block in range(start, stop):
            base = block * tile
            inside = (lane >= base) & (lane < base + tile)
            diagonal = ahead if block > start else columns(rows[block], base)
            follow = block + 1 < stop
            if follow:
                beside = columns(rows[block], base + tile)
                under = columns(rows[block + 1], base)
                ahead = columns(rows[block + 1], base + tile)
            pivots = jnp.ones((tile, size), f32)
            inverses, ratios, known = [], [], {}
            for t in range(tile):
                pivot = spread(diagonal[t], t)
                pivots = jnp.where(level == t, pivot, pivots)
                inverses.append(1.0 / pivot)
                ratios.append(jnp.where(level > t, diagonal[t], 0.0) * inverses[t])
                for c in range(t + 1, tile):
                    known[t, c] = spread(diagonal[c], t)
                    diagonal[c] = diagonal[c] - ratios[t] * known[t, c]
            if follow:
                for t in range(tile):
                    ratio = under[t] * inverses[t]
                    for c in range(t + 1, tile):
                        under[c] = under[c] - ratio * known[t, c]
                    for c in range(tile):
                        across = spread(beside[c], t)
                        ahead[c] = ahead[c] - ratio * across
                        beside[c] = beside[c] - ratios[t] * across
            panel = jnp.where(inside, jnp.where(lane - base == level, 1.0, 0.0), rows[block])
            spreads = []
            for t in range(tile):
                spreads.append(spread(panel, t))
                panel = panel - ratios[t] * spreads[t]
            panels[block], scales[block] = panel, pivots
            for below in range(block + 1, stop):
                multiples = columns(rows[below], base)
                row = jnp.where(inside, 0.0, rows[below])
                for t in range(tile):
                    ratio = multiples[t] * inverses[t]
                    row = row - ratio * spreads[t]
                    for c in range(t + 1, tile):
                        multiples[c] = multiples[c] - ratio * known[t, c]
                rows[below] = row
        if stop < count:
            first, last = start * tile, stop * tile
            done = range(start, stop)
            wide = [
                jnp.where((lane < last) & (lane > b * tile + level), 0.0, panels[b]) for b in done
            ]
            scaled = [panels[b] / scales[b] for b in done]
            change = lax.dot_general(
                jnp.concatenate(scaled, axis=0),
                jnp.concatenate(wide, axis=0),
                contract_rows,
                precision=highest,
                preferred_element_type=f32,
            )
            for below in range(stop, count):
                kept = jnp.where((lane >= first) & (lane < last), 0.0, rows[below])
                rows[below] = kept - change[below * tile : (below + 1) * tile]
    return jnp.concatenate(
        [
            jnp.where(lane <= b * tile + level, panels[b], 0.0) * lax.rsqrt(scales[b])
            for b in range(count)
        ],
        axis=0,
    )


def gram_of(rows):
    return lax.dot_general(
        rows, rows, contract_rows, precision=highest, preferred_element_type=f32
    )


def gram_kernel(image_ref, gram_ref):
    gram_ref[...] = gram_of(image_ref[...])


def outputs_kernel(
    gram_ref, image_ref, image_other_ref, own_ref, other_ref, basis_ref, core_ref, basis_own_ref
):
    mode_index = lax.axis_index("mode")
    image_other = image_other_ref[...]
    inverse = inverse_factor(gram_ref[...] + gram_of(image_other))
    inverse_high, inverse_low = two_parts(inverse)

    def basis_of(image):
        high, low = two_parts(image)
        small = dot(high, inverse_low, contract_last) + dot(low, inverse_high, contract_last)
        return dot(high, inverse_high, contract_last) + small

    basis_own = basis_of(image_ref[...])
    basis_own_ref[...] = basis_own
    rows = basis_ref.shape[0]
    place = pl.multiple_of(mode_index // 2 * rows, rows)
    basis_ref[...] = basis_own_ref[pl.ds(place, rows), :]
    core_ref[...] = dot(own_ref[...], basis_own.astype(bf16), contract_rows) + dot(
        other_ref[...], basis_of(image_other).astype(bf16), contract_rows
    )


def shards(tensor, start_block):
    row_count, slab_columns = tensor.shape
    modes = lax.axis_size("mode")
    chips = modes // 2
    far_mask = chips // 2
    chip_columns = slab_columns // chips
    own_columns = chip_columns // 2
    held_rows = chips * row_count
    rank = start_block.shape[1]

    masks = [(0, 0), (far_mask, 1), (1, far_mask)] if far_mask > 1 else [(0, 0), (1, 1)]
    masks += [(mask, mask) for mask in reversed(range(2, chips)) if mask != far_mask]

    def split(source, some):
        return pl.pallas_call(
            functools.partial(split_kernel, some),
            out_shape=[pltpu.VMEM((row_count, chip_columns), bf16)] * len(some),
            in_specs=[pl.BlockSpec(memory_space=pl.ANY)],
            out_specs=vmem_specs(len(some)),
            scratch_shapes=[pltpu.SemaphoreType.DMA((len(some) * row_count // 16,))],
        )(source)

    (first,) = split(tensor, masks[1:2])
    first, tensor = lax.optimization_barrier((first, tensor))
    rest = split(tensor, masks[:1] + masks[2:])
    blocks = [rest[0], first, *rest[1:]]
    for place in range(1, chips):
        even_mask, odd_mask = masks[place]
        blocks[place] = exchange(blocks[place], (0, even_mask), (0, odd_mask))

    inner, inner_low, held, own_half, away_half = pl.pallas_call(
        functools.partial(inner_kernel, masks),
        out_shape=(
            pltpu.VMEM((rank, chip_columns), f32),
            pltpu.VMEM((rank, chip_columns), bf16),
            pltpu.VMEM((held_rows, chip_columns), bf16),
            pltpu.VMEM((held_rows, own_columns), bf16),
            pltpu.VMEM((held_rows, own_columns), bf16),
        ),
        in_specs=vmem_specs(1 + chips),
        out_specs=tuple(vmem_specs(5)),
    )(*in_vmem(start_block, *blocks))
    inner_other = swap_cores(inner_low)
    other_half = swap_cores(away_half)

    image = pl.pallas_call(
        image_kernel,
        out_shape=pltpu.VMEM((held_rows, rank), bf16),
        in_specs=vmem_specs(3),
        out_specs=vmem_specs(1)[0],
    )(*in_vmem(held, inner, inner_other))
    image = sum_over_chips(image)
    image_other = swap_cores(image)
    gram = pl.pallas_call(
        gram_kernel,
        out_shape=pltpu.VMEM((rank, rank), f32),
        in_specs=vmem_specs(1),
        out_specs=vmem_specs(1)[0],
    )(*in_vmem(image))

    return pl.pallas_call(
        outputs_kernel,
        out_shape=(
            jax.ShapeDtypeStruct((row_count, rank), f32),
            jax.ShapeDtypeStruct((own_columns, rank), f32),
        ),
        in_specs=vmem_specs(5),
        out_specs=tuple(vmem_specs(2)),
        scratch_shapes=[pltpu.VMEM((held_rows, rank), f32)],
    )(*in_vmem(gram, image, image_other, own_half, other_half))


def solution(mesh):
    placed = (P("mode", "slab"), P())
    return jax.shard_map(
        shards,
        mesh=mesh,
        in_specs=placed,
        out_specs=(P("mode", None), P(("slab", "mode"), None)),
        check_vma=False,
    )
```
